32 devices in a mesh: tm: 8 (over z, x), panel: 4 (over y, core).
Axes of the slice: x: 2, y: 2, z: 4, core: 2. Of those that a mesh axis runs over, the one named last changes fastest.
Arguments:
- design: bfloat16 [2048, 7680], P('tm', 'panel'), may hold values from -6 to 6
- partials: bfloat16 [2048, 64], P('tm'), may hold values from -0.119628906 to 0.119628906
- observed: bfloat16 [2048], P('tm'), may hold values from -6 to 6
- arc_of_row: int32 [2048, 1], replicated, may hold values from 0 to 7, as said below
- autoreg: float32 [8], replicated, may hold values from -0.55 to 0.5
- movavg: float32 [8], replicated, may hold values from 0.3 to 0.9
Outputs:
- normal: float32 [7680, 7680], P('tm', 'panel')
- right_hand: float32 [7680], P('panel')
The draws below stay inside these ranges and needn't reach their ends.
Inputs may be any that keep to these rules, and one draw needn't show every extreme that they name: arc_of_row never falls along the epochs and names every arc; arcs 2b and 2b + 1 together have 2 * 256 epochs, one of them 384 // 3 to 160 epochs and the other 352 to 384; one arc has exactly 384 epochs and its partner exactly 128, so that at most 48 rows of one device belong to one arc, and every device holds exactly 48 rows of the longest arc; arc a is held by index a of tm.
All inputs are finite; a program needn't handle non-finite values.
Results may differ from the reference program's by a relative error of at most 0.02.
Values may be sent and summed in bfloat16 or wider, within the bound.
No kernel may reach another device: no remote copies, remote signals or barrier semaphores. Data moves between devices by JAX's collectives and lax.ppermute only.
A program may use at most 192 MiB of HBM per device.

```python
import jax
import jax.numpy as jnp
from jax import lax

NC = 7680
NA = 64
ROW_DEV = 256
ROWS = 2048
ARCS = 8
SLOTS = 384
N_TM = 8


def draw_arc_of_row(key, part):
    half_rows = ROW_DEV // 2
    least_shift = 3 * half_rows // 4
    pair_count = ARCS // 2
    key_shift = jax.random.fold_in(key, 11)
    key_pick = jax.random.fold_in(key, 12)
    key_sign = jax.random.fold_in(key, 13)
    key_signs = jax.random.fold_in(key, 14)
    magnitude = jax.random.randint(key_shift, (pair_count,), least_shift, half_rows + 1)
    signs = jax.random.randint(key_signs, (pair_count,), 0, 2) * 2 - 1
    shifts = magnitude * signs
    chosen = jax.random.randint(key_pick, (), 0, pair_count)
    sign_value = jax.random.randint(key_sign, (), 0, 2) * 2 - 1
    shifts = jnp.where(jnp.arange(pair_count) == chosen, sign_value * half_rows, shifts)
    lengths = jnp.stack([ROW_DEV + shifts, ROW_DEV - shifts], axis=1).reshape(ARCS)
    ends = jnp.cumsum(lengths)
    epochs = jnp.arange(ROWS, dtype=jnp.int32)
    arcs = jnp.sum((epochs[:, None] >= ends[None, :]).astype(jnp.int32), axis=1)
    return arcs.astype(jnp.int32).reshape(ROWS, 1)


def noise_coefficients(key):
    key_ar = jax.random.fold_in(key, 21)
    key_ma = jax.random.fold_in(key, 22)
    ma_values = jax.random.uniform(key_ma, (ARCS,), jnp.float32, 0.3, 0.9)
    ar_values = jax.random.uniform(key_ar, (ARCS,), jnp.float32, -0.5, 0.5)
    return (ar_values, ma_values)


def draw_autoreg(key, part):
    ar_values, ma_values = noise_coefficients(key)
    return ar_values.astype(jnp.float32)


def draw_movavg(key, part):
    ar_values, ma_values = noise_coefficients(key)
    return ma_values.astype(jnp.float32)


def shard_levels(stream_key, extent, pieces, low, high):
    gain = 1.0
    for axis_at, parts in pieces:
        draws = jax.random.uniform(jax.random.fold_in(jax.random.fold_in(stream_key, 6), axis_at), (parts,), jnp.float32, low / len(pieces), high / len(pieces))
        gain = gain * jnp.repeat(jnp.exp(draws), extent[axis_at] // parts).reshape((-1,) + (1,) * (len(extent) - 1 - axis_at))
    return gain


def centred(key, extent, width, most, split=(), kind=jnp.bfloat16):
    loudness = shard_levels(key, extent, split, -0.22, 0.18) if split else 1.0
    array = jax.random.normal(key, extent, jnp.float32) * width * loudness
    return jnp.minimum(jnp.maximum(array, -most), most).astype(kind)


def setup_inputs(seed: int = 0) -> dict:
    key_of = jax.random.split(jax.random.key(seed), 7)
    return {
        "design": centred(key_of[0], (ROWS, NC), 1.0, 6.0, ((0, 8), (1, 4))),
        "partials": centred(key_of[1], (ROWS, NA), 0.02, 0.119628906, ((0, 8),)),
        "observed": centred(key_of[2], (ROWS,), 1.0, 6.0, ((0, 8),)),
        "arc_of_row": draw_arc_of_row(jax.random.fold_in(key_of[6], 71), 0),
        "autoreg": draw_autoreg(jax.random.fold_in(key_of[6], 71), 0),
        "movavg": draw_movavg(jax.random.fold_in(key_of[6], 71), 0),
    }


def whiten_matrix(order_row, order_col, usable_row, usable_col, ar_value, ma_value):
    spacing = order_row[:, None] - order_col[None, :]
    lag_steps = jnp.maximum(spacing - 1, 0)
    parity = (lag_steps % 2).astype(jnp.float32)
    flip_sign = 1.0 - 2.0 * parity
    decayed = -(ar_value + ma_value) * flip_sign * jnp.exp(lag_steps.astype(jnp.float32) * jnp.log(ma_value))
    entry = jnp.where(spacing == 0, jnp.float32(1.0), decayed)
    allowed = usable_row[:, None] & usable_col[None, :] & (spacing >= 0)
    return jnp.where(allowed, entry, jnp.float32(0.0)).astype(jnp.bfloat16)

def eliminate(whitener, rows_design, rows_params, rows_obs, scale):
    white_design = jnp.dot(whitener.astype(jnp.float32), rows_design.astype(jnp.float32), preferred_element_type=jnp.float32)
    white_params = jnp.dot(whitener.astype(jnp.float32), rows_params.astype(jnp.float32), preferred_element_type=jnp.float32)
    white_obs = jnp.dot(whitener.astype(jnp.float32), rows_obs.astype(jnp.float32), preferred_element_type=jnp.float32)
    param_count = rows_params.shape[1]
    param_gram = jnp.dot(white_params.T, white_params, precision=lax.Precision.HIGHEST) + jnp.eye(param_count, dtype=jnp.float32)
    factor = jnp.linalg.cholesky(param_gram)
    basis = lax.linalg.triangular_solve(factor, white_params.T, left_side=True, lower=True)
    arc_terms = jnp.dot(basis, white_design, precision=lax.Precision.HIGHEST)
    arc_rhs = jnp.dot(basis, white_obs, precision=lax.Precision.HIGHEST)
    right_part = (jnp.dot(white_design.T, white_obs, precision=lax.Precision.HIGHEST) - jnp.dot(arc_terms.T, arc_rhs, precision=lax.Precision.HIGHEST)) * scale
    return (white_design.astype(jnp.bfloat16), arc_terms.astype(jnp.bfloat16), right_part)

def reference(design, partials, observed, arc_of_row, autoreg, movavg):
    arc_ids = arc_of_row[:, 0]
    pad_design = jnp.concatenate([design, jnp.zeros((1, NC), jnp.bfloat16)], axis=0)
    pad_params = jnp.concatenate([partials, jnp.zeros((1, NA), jnp.bfloat16)], axis=0)
    pad_obs = jnp.concatenate([observed, jnp.zeros((1,), jnp.bfloat16)], axis=0)
    position = jnp.arange(SLOTS, dtype=jnp.int32)
    scale = 1.0 / ROWS

    def one_arc(running, arc_id):
        normal, right_hand = running
        arc_length = jnp.sum((arc_ids == arc_id).astype(jnp.int32))
        arc_start = jnp.sum((arc_ids < arc_id).astype(jnp.int32))
        usable = position < arc_length
        epochs = (arc_start + position).astype(jnp.int32)
        row_index = (epochs % N_TM * ROW_DEV + epochs // N_TM).astype(jnp.int32)
        picked = jnp.where(usable, row_index, jnp.int32(ROWS)).astype(jnp.int32)
        whitener = whiten_matrix(position, position, usable, usable, autoreg[arc_id], movavg[arc_id])
        design_bf, terms_bf, right_part = eliminate(whitener, pad_design[picked], pad_params[picked], pad_obs[picked], scale)
        partial_value = (jnp.dot(design_bf.T.astype(jnp.float32), design_bf.astype(jnp.float32), preferred_element_type=jnp.float32) - jnp.dot(terms_bf.T.astype(jnp.float32), terms_bf.astype(jnp.float32), preferred_element_type=jnp.float32)) * scale
        rounded = lax.optimization_barrier(partial_value.astype(jnp.bfloat16))
        return ((normal + rounded.astype(jnp.float32), right_hand + right_part), None)
    start_state = (jnp.zeros((NC, NC), jnp.float32), jnp.zeros((NC,), jnp.float32))
    (normal, right_hand), _ = lax.scan(one_arc, start_state, jnp.arange(ARCS, dtype=jnp.int32))
    return (normal, right_hand)
```

```python
import functools

import jax
import jax.numpy as jnp
from jax import lax
from jax.experimental import pallas as pl
from jax.experimental.pallas import tpu as pltpu
from jax.sharding import PartitionSpec as P

AXES = ("tm", "panel")
HIGHEST = lax.Precision.HIGHEST
ROWS_ACROSS = (((0,), (0,)), ((), ()))
SWEEPS = 16
EXTRA = 16
HBM = pl.BlockSpec(memory_space=pl.ANY)
SMEM = pl.BlockSpec(memory_space=pltpu.SMEM)
FROM_Z = ((1, 3, 0, 2), (2, 0, 3, 1), (3, 2, 1, 0))
SEND_Z = (((1, 0), (3, 1), (0, 2), (2, 3)), ((2, 0), (0, 1), (3, 2), (1, 3)), ((1, 0), (3, 1), (0, 2), (2, 3)))


def params(mib, **more):
    return pltpu.CompilerParams(vmem_limit_bytes=mib * 1024 * 1024, **more)


def whiten_kernel(
    shard_ref, length_ref, gain_ref, log_ref, slots_ref, gram_ref, across_ref, square_ref, obs_ref, held
):
    tile_count, pair_rows, width = slots_ref.shape
    size = tile_count * pair_rows
    shift = pair_rows.bit_length() - 1
    pair = pl.program_id(0)
    length = length_ref[pair]

    def epoch(shape, axis):
        at = lax.broadcasted_iota(jnp.int32, shape, axis)
        return jnp.bitwise_and(at, pair_rows - 1) * tile_count + jnp.right_shift(at, shift)

    epoch_row, epoch_col = epoch((size, 1), 0), epoch((1, size), 1)
    first_row = jnp.where(epoch_row < length, 1, 0)
    first_col = jnp.where(epoch_col < length, 1, 0)
    gain = jnp.where(epoch_row < length, gain_ref[2 * pair], gain_ref[2 * pair + 1])
    log_ma = jnp.where(epoch_row < length, log_ref[2 * pair], log_ref[2 * pair + 1])
    spacing = epoch_row - epoch_col
    lag = jnp.maximum(spacing - 1, 0)
    size_of = gain * jnp.exp(lag.astype(jnp.float32) * log_ma)
    decayed = jnp.where(jnp.bitwise_and(lag, 1) == 1, size_of, -size_of)
    entry = jnp.where(spacing == 0, jnp.float32(1.0), decayed)
    allowed = (first_row == first_col) & (spacing >= 0)
    whitener = jnp.where(allowed, entry, jnp.float32(0.0)).astype(jnp.bfloat16)

    for n in range(tile_count):
        at = pl.multiple_of(shard_ref[n] * pair_rows, pair_rows)
        held[pl.ds(at, pair_rows), :] = slots_ref[n].astype(jnp.float32)
    rows = held[...]
    obs_ref[0] = rows.T[width // 2 : width // 2 + EXTRA].astype(jnp.bfloat16)
    lane = lax.broadcasted_iota(jnp.int32, (size, width), 1)
    in_first = jnp.where(lane < width // 2, 1, 0)
    rows = jnp.where(in_first == 1, rows, pltpu.roll(rows, width // 2, axis=1))
    rows = jnp.where(in_first == first_row, rows, 0.0).astype(jnp.bfloat16)
    white = jnp.dot(whitener, rows, preferred_element_type=jnp.float32)
    eye = lax.broadcasted_iota(jnp.int32, (width, width), 0) == lax.broadcasted_iota(
        jnp.int32, (width, width), 1
    )
    gram_ref[0] = lax.dot_general(
        white, white, ROWS_ACROSS, precision=HIGHEST, preferred_element_type=jnp.float32
    ) + jnp.where(eye, 1.0, 0.0)
    high = white.astype(jnp.bfloat16)
    rest = white - high.astype(jnp.float32)
    middle = rest.astype(jnp.bfloat16)
    low = (rest - middle.astype(jnp.float32)).astype(jnp.bfloat16)
    across_ref[0] = sum(
        lax.dot_general(part, whitener, ROWS_ACROSS, preferred_element_type=jnp.float32)
        for part in (low, middle, high)
    )
    square_ref[0] = lax.dot_general(
        whitener, whitener, ROWS_ACROSS, preferred_element_type=jnp.float32
    )


def invert_kernel(first, count, gram_ref, out_ref):
    size, arcs, _ = gram_ref.shape
    lane = lax.broadcasted_iota(jnp.int32, (arcs, size), 1)
    source = gram_ref
    for k in range(first, first + count):
        row = source[k]
        here = lane == k
        inverse = 1.0 / row[:, k : k + 1]
        scaled = row * inverse
        for i in [(k + 1 + n) % size for n in range(size - 1)]:
            column = row[:, i : i + 1]
            out_ref[i] = jnp.where(here, column * inverse, source[i] - column * scaled)
        out_ref[k] = jnp.where(here, -inverse, scaled)
        source = out_ref


def middle_kernel(across_ref, minus_inverse_ref, square_ref, obs_ref, out_ref):
    size = square_ref.shape[1]
    across = across_ref[0]
    reduced = jnp.dot(
        minus_inverse_ref[0], across, precision=HIGHEST, preferred_element_type=jnp.float32
    )
    whole = square_ref[0] + lax.dot_general(
        across, reduced, ROWS_ACROSS, precision=HIGHEST, preferred_element_type=jnp.float32
    )
    high = whole.astype(jnp.bfloat16)
    rest = whole - high.astype(jnp.float32)
    middle = rest.astype(jnp.bfloat16)
    low = (rest - middle.astype(jnp.float32)).astype(jnp.bfloat16)
    obs = obs_ref[0]
    value = sum(
        jnp.dot(obs, part, preferred_element_type=jnp.float32) for part in (low, middle, high)
    )
    value_high = value.astype(jnp.bfloat16)
    rest = value - value_high.astype(jnp.float32)
    value_middle = rest.astype(jnp.bfloat16)
    value_low = rest - value_middle.astype(jnp.float32)
    at = lax.broadcasted_iota(jnp.int32, (EXTRA, size), 0)
    parts = jnp.where(
        at == 0,
        value_high.astype(jnp.float32),
        jnp.where(at == 1, value_middle.astype(jnp.float32), jnp.where(at == 2, value_low, 0.0)),
    )
    out_ref[0, :size] = high
    out_ref[0, size : 2 * size] = middle
    out_ref[0, 2 * size :] = parts.astype(jnp.bfloat16)


def pair_matrices(slots, shard, arc_of_row, autoreg, movavg):
    tile_count, rows_dev, width = slots.shape
    param_count = width // 2
    pair_rows = 2 * rows_dev // tile_count
    pair_count = rows_dev // pair_rows
    size = tile_count * pair_rows
    arc_count = 2 * pair_count
    first = 2 * jnp.arange(pair_count, dtype=jnp.int32)
    lengths = jnp.sum((arc_of_row == first[None, :]).astype(jnp.int32), axis=0)

    def per_pair(*shape):
        return pl.BlockSpec((1, *shape), lambda b: (b, 0, 0))

    gram, across, square, obs = pl.pallas_call(
        whiten_kernel,
        grid=(pair_count,),
        in_specs=[SMEM] * 4 + [pl.BlockSpec((tile_count, pair_rows, width), lambda b: (0, b, 0))],
        out_specs=[
            per_pair(width, width),
            per_pair(width, size),
            per_pair(size, size),
            per_pair(EXTRA, size),
        ],
        out_shape=[
            jax.ShapeDtypeStruct((pair_count, width, width), jnp.float32),
            jax.ShapeDtypeStruct((pair_count, width, size), jnp.float32),
            jax.ShapeDtypeStruct((pair_count, size, size), jnp.float32),
            jax.ShapeDtypeStruct((pair_count, EXTRA, size), jnp.bfloat16),
        ],
        scratch_shapes=[pltpu.VMEM((size, width), jnp.float32)],
        compiler_params=params(40),
        name="whiten",
    )(shard, lengths, autoreg + movavg, jnp.log(movavg), slots)
    blocks = jnp.stack(
        [gram[:, :param_count, :param_count], gram[:, param_count:, param_count:]], axis=1
    ).reshape(arc_count, param_count, param_count)
    minus = blocks.transpose(1, 0, 2)
    for first in range(0, param_count, SWEEPS):
        minus = pl.pallas_call(
            functools.partial(invert_kernel, first, SWEEPS),
            out_shape=jax.ShapeDtypeStruct(minus.shape, jnp.float32),
            name="invert",
        )(minus)
    minus = minus.transpose(1, 0, 2).reshape(pair_count, 2, param_count, param_count)
    nothing = jnp.zeros((pair_count, param_count, param_count), jnp.float32)
    minus = jnp.concatenate(
        [
            jnp.concatenate([minus[:, 0], nothing], axis=2),
            jnp.concatenate([nothing, minus[:, 1]], axis=2),
        ],
        axis=1,
    )
    return pl.pallas_call(
        middle_kernel,
        grid=(pair_count,),
        in_specs=[per_pair(width, size), per_pair(width, width), per_pair(size, size), per_pair(EXTRA, size)],
        out_specs=per_pair(2 * size + EXTRA, size),
        out_shape=jax.ShapeDtypeStruct((pair_count, 2 * size + EXTRA, size), jnp.bfloat16),
        compiler_params=params(40),
        name="middle",
    )(across, minus, square, obs)


def pack_kernel(count, width, meta_ref, *refs):
    slots, out, held, sems = refs[:count], refs[count], refs[count + 1], refs[count + 2]
    start = pl.multiple_of(meta_ref[1], 128)

    @pl.when(meta_ref[0] == 1)
    def _():
        into, back, at = [], [], 0
        for n, slot in enumerate(slots):
            here = pl.ds(at, slot.shape[0])
            columns = slot.at[:, pl.ds(start, width)]
            into.append(pltpu.make_async_copy(columns, held.at[here], sems.at[0, n]))
            back.append(pltpu.make_async_copy(held.at[here], out.at[here], sems.at[1, n]))
            at += slot.shape[0]
        for copy in into:
            copy.start()
        for first, second in zip(into, back):
            first.wait()
            second.start()
        for copy in back:
            copy.wait()


def pack(meta, slots, width):
    rows = sum(slot.shape[0] for slot in slots)
    return pl.pallas_call(
        functools.partial(pack_kernel, len(slots), width),
        in_specs=[SMEM] + [HBM] * len(slots),
        out_specs=HBM,
        out_shape=jax.ShapeDtypeStruct((rows, width), slots[0].dtype),
        scratch_shapes=[
            pltpu.VMEM((rows, width), slots[0].dtype),
            pltpu.SemaphoreType.DMA((2, len(slots))),
        ],
        name="pack",
    )(meta, *slots)


def middle_rows_kernel(scale, shard_ref, mid_ref, *refs):
    *slots, out, rhs, panel, middle = refs
    pair_rows = slots[0].shape[0]
    size = len(slots) * pair_rows

    def place(n):
        return pl.ds(pl.multiple_of(shard_ref[n] * pair_rows, pair_rows), pair_rows)

    for n, slot in enumerate(slots):
        panel[place(n), :] = slot[...]
    product = jnp.dot(mid_ref[0], panel[...], preferred_element_type=jnp.float32)
    middle[...] = (product[:size] + product[size : 2 * size]).astype(jnp.bfloat16)
    for n in range(len(slots)):
        out[n] = middle[place(n), :]
    rhs_here = jnp.sum(product[2 * size :], axis=0, keepdims=True) * scale

    @pl.when(pl.program_id(0) == 0)
    def _():
        rhs[...] = rhs_here

    @pl.when(pl.program_id(0) > 0)
    def _():
        rhs[...] += rhs_here


def middle_rows(shard, mids, first_pair, slots, pair_rows, scale):
    rows, width = slots[0].shape
    pair_count = rows // pair_rows
    size = len(slots) * pair_rows
    return pl.pallas_call(
        functools.partial(middle_rows_kernel, scale),
        grid=(pair_count,),
        in_specs=[SMEM, pl.BlockSpec((1, 2 * size + EXTRA, size), lambda b: (b + first_pair, 0, 0))]
        + [pl.BlockSpec((pair_rows, width), lambda b: (b, 0))] * len(slots),
        out_specs=[
            pl.BlockSpec((len(slots), pair_rows, width), lambda b: (0, b, 0)),
            pl.BlockSpec((1, width), lambda b: (0, 0)),
        ],
        out_shape=[
            jax.ShapeDtypeStruct((len(slots), rows, width), jnp.bfloat16),
            jax.ShapeDtypeStruct((1, width), jnp.float32),
        ],
        scratch_shapes=[
            pltpu.VMEM((size, width), jnp.bfloat16),
            pltpu.VMEM((size, width), jnp.bfloat16),
        ],
        compiler_params=params(48),
        cost_estimate=pl.CostEstimate(
            flops=2 * pair_count * (2 * size + EXTRA) * size * width,
            bytes_accessed=2 * len(slots) * rows * width * 2,
            transcendentals=0,
        ),
        name="middle_rows",
    )(shard, mids, *slots)


def tile_kernel(places, block_columns, scale, meta_ref, *refs):
    groups = 1 + max(group for group, _ in places)
    blocks, refs = refs[: 4 * groups], refs[4 * groups :]
    *middles, out, block, turned, sems = refs
    rows = middles[0].shape[1]
    step = middles[0].shape[2]

    def copies(kind):
        return [
            pltpu.make_async_copy(
                blocks[4 * group + kind].at[pl.ds(at, rows)],
                block.at[pl.ds(n * rows, rows)],
                sems.at[n],
            )
            for n, (group, at) in enumerate(places)
        ]

    @pl.when(pl.program_id(0) == 0)
    def _():
        for kind in range(4):

            @pl.when(meta_ref[1] == kind)
            def _(kind=kind):
                for copy in copies(kind):
                    copy.start()

        for n, copy in enumerate(copies(0)):
            copy.wait()
            turned[:, n * rows : (n + 1) * rows] = block[n * rows : (n + 1) * rows, :].T

    middle = jnp.concatenate([one[...].reshape(-1, step) for one in middles], axis=0)
    offset = pl.multiple_of(meta_ref[0], 64)
    out[...] = (
        jnp.dot(
            turned[pl.ds(offset, block_columns), :], middle, preferred_element_type=jnp.float32
        )
        * scale
    )


def tile(meta, middles, places, blocks, block_columns, scale, step):
    count, rows, width = middles[0].shape
    payload = blocks[0][0].shape[1]
    total = count * rows * len(middles)
    return pl.pallas_call(
        functools.partial(tile_kernel, tuple(places), block_columns, scale),
        grid=(pl.cdiv(width, step),),
        in_specs=[SMEM]
        + [HBM] * (4 * len(blocks))
        + [pl.BlockSpec((count, rows, step), lambda j: (0, 0, j))] * len(middles),
        out_specs=pl.BlockSpec((block_columns, step), lambda j: (0, j)),
        out_shape=jax.ShapeDtypeStruct((block_columns, width), jnp.float32),
        scratch_shapes=[
            pltpu.VMEM((total, payload), jnp.bfloat16),
            pltpu.VMEM((payload, total), jnp.bfloat16),
            pltpu.SemaphoreType.DMA((len(places),)),
        ],
        compiler_params=params(56),
        cost_estimate=pl.CostEstimate(
            flops=2 * block_columns * width * total,
            bytes_accessed=block_columns * width * 4 + total * (payload + width) * 2,
            transcendentals=0,
        ),
        name="tile",
    )(meta, *[one for four in blocks for one in four], *middles)


def tie(value, *others):
    return lax.optimization_barrier((value, *others))[0]


def block_body(design, partials, observed, arc_of_row, autoreg, movavg):
    tile_count, panel_count = lax.axis_size("tm"), lax.axis_size("panel")
    rows_dev, width = design.shape
    block_columns = width * panel_count // tile_count
    payload = pl.cdiv(block_columns, 128) * 128
    pair_rows = 2 * rows_dev // tile_count
    scale = 1.0 / (rows_dev * tile_count)
    t, p = lax.axis_index("tm"), lax.axis_index("panel")
    z, x, y, core = t // 2, t % 2, p // 2, p % 2
    near, same_core = y == z // 2, core == z % 2

    def along_z(value, turn):
        pairs = [(2 * s + i, 2 * d + i) for s, d in SEND_Z[turn] for i in range(2)]
        return lax.ppermute(value, "tm", pairs)

    def across_x(value):
        return lax.ppermute(value, "tm", [(s, s ^ 1) for s in range(tile_count)])

    def hop(value, go):
        pairs = []
        for s in range(tile_count * panel_count):
            sz, sy, sc = s // 8, s // 2 % 2, s % 2
            to = go(sy == sz // 2, sc == sz % 2)
            if to is not None:
                pairs.append((s, s - s % 4 + (sy ^ to[0]) * 2 + (sc ^ to[1])))
        return lax.ppermute(value, AXES, pairs)

    line = [z] + [jnp.array(FROM_Z[turn], jnp.int32)[z] for turn in range(3)]
    shard = jnp.stack([2 * s + i for s in line for i in (x, 1 - x)]).astype(jnp.int32)

    sent = jnp.concatenate([partials, jnp.broadcast_to(observed[:, None], partials.shape)], axis=1)
    sent = jnp.stack([sent, across_x(sent)])
    sent_1, sent_2 = along_z(sent, 0), along_z(sent, 1)
    half = rows_dev // 2
    own_a, own_b = design[:half], design[half:]
    z1a = along_z(own_a, 0)
    x0a = across_x(own_a)
    z2a = along_z(own_a, 1)
    x0b = across_x(own_b)
    sent = jnp.concatenate([sent, sent_1, sent_2, along_z(sent_1, 2)])
    mids = pair_matrices(sent, shard, arc_of_row, autoreg, movavg)
    z3a = along_z(z1a, 2)
    z1b = along_z(tie(own_b, z1a), 0)
    z2b = along_z(tie(own_b, z2a), 1)
    x1a = across_x(tie(z1a, x0a))
    x2a = across_x(tie(z2a, x0b))
    z3b = along_z(z1b, 2)
    x3a = across_x(tie(z3a, x1a))
    x1b = across_x(tie(z1b, x2a))
    x2b = across_x(tie(z2b, x3a))
    x3b = across_x(tie(z3b, x1b))

    pack_meta = jnp.stack([(near & same_core).astype(jnp.int32), x * (width - payload)])

    def spread(*slots):
        mine = pack(pack_meta, slots, payload)
        over = hop(mine, lambda near, same: (1, 0) if near and same else None)
        beside = hop(mine, lambda near, same: (0, 1) if near and same else None)
        both = hop(over, lambda near, same: (0, 1) if not near and same else None)
        return mine, over, beside, both

    groups = [
        spread(own_a, own_b, x0a, x0b, z1a, z2a),
        spread(z3a, x1a, x2a, x3a, z1b, z2b),
        spread(z3b, x1b, x2b),
        spread(x3b),
    ]
    slots_a = (own_a, x0a, z1a, x1a, z2a, x2a, z3a, x3a)
    slots_b = (own_b, x0b, z1b, x1b, z2b, x2b, z3b, x3b)
    places_a = [(0, 0), (0, 2), (0, 4), (1, 1), (0, 5), (1, 2), (1, 0), (1, 3)]
    places_b = [(0, 1), (0, 3), (1, 4), (2, 1), (1, 5), (2, 2), (2, 0), (3, 0)]
    places = [(group, at * half) for group, at in places_a + places_b]

    kind = jnp.where(same_core, jnp.where(near, 0, 1), jnp.where(near, 2, 3))
    meta = jnp.stack([x * (payload - block_columns), kind]).astype(jnp.int32)
    middle_a, rhs_a = middle_rows(shard, mids, 0, slots_a, pair_rows, scale)
    middle_b, rhs_b = middle_rows(shard, mids, half // pair_rows, slots_b, pair_rows, scale)
    normal = tile(meta, (middle_a, middle_b), places, groups, block_columns, scale, 512)
    return normal, (rhs_a + rhs_b)[0]


def line_body(design, partials, observed, arc_of_row, autoreg, movavg):
    tile_count = lax.axis_size("tm")
    rows_dev, width = design.shape
    pair_rows = 2 * rows_dev // tile_count
    pair_count = rows_dev // pair_rows
    size = tile_count * pair_rows
    scale = 1.0 / (rows_dev * tile_count)
    sent = jnp.concatenate([partials, jnp.broadcast_to(observed[:, None], partials.shape)], axis=1)
    sent = lax.all_gather(sent, "tm", axis=0, tiled=False)
    shard = jnp.arange(tile_count, dtype=jnp.int32)
    mids = pair_matrices(sent, shard, arc_of_row, autoreg, movavg)
    panel = lax.all_gather(design, "tm", axis=0, tiled=False)
    whole_rows = lax.all_gather(design, "panel", axis=1, tiled=True)
    block = lax.all_to_all(whole_rows, "tm", split_axis=1, concat_axis=0, tiled=True)
    block = block.reshape(tile_count, rows_dev, -1)

    def one_pair(sums, pair):
        def rows_of(values):
            here = lax.dynamic_slice_in_dim(values, pair * pair_rows, pair_rows, 1)
            return here.reshape(size, values.shape[2])

        product = jnp.dot(mids[pair], rows_of(panel), preferred_element_type=jnp.float32)
        middle = (product[:size] + product[size : 2 * size]).astype(jnp.bfloat16)
        here = lax.dot_general(
            rows_of(block), middle, ROWS_ACROSS, preferred_element_type=jnp.float32
        )
        return (sums[0] + here, sums[1] + jnp.sum(product[2 * size :], axis=0)), None

    start = (jnp.zeros((block.shape[2], width), jnp.float32), jnp.zeros((width,), jnp.float32))
    (normal, right_hand), _ = lax.scan(one_pair, start, jnp.arange(pair_count))
    return normal * scale, right_hand * scale


def solution(mesh):
    in_specs = (P("tm", "panel"), P("tm", None), P("tm"), P(), P(), P())
    out_specs = (P("tm", "panel"), P("panel"))
    body = block_body if (mesh.shape["tm"], mesh.shape["panel"]) == (8, 4) else line_body
    return jax.shard_map(body, mesh=mesh, in_specs=in_specs, out_specs=out_specs, check_vma=False)
```

```python
import functools

import jax
import jax.numpy as jnp
from jax import lax
from jax.experimental import pallas as pl
from jax.experimental.pallas import tpu as pltpu
from jax.sharding import PartitionSpec as P

AXES = ("tm", "panel")
HIGHEST = lax.Precision.HIGHEST
ROWS_ACROSS = (((0,), (0,)), ((), ()))
EXTRA = 128
HBM = pl.BlockSpec(memory_space=pl.ANY)
SMEM = pl.BlockSpec(memory_space=pltpu.SMEM)
SEND_Z = (((1, 0), (3, 1), (0, 2), (2, 3)), ((2, 0), (0, 1), (3, 2), (1, 3)), ((1, 0), (3, 1), (0, 2), (2, 3)), ((3, 0), (2, 1), (1, 2), (0, 3)))


COST = 1e9
SMALL = 0.5
ROWS = 12


def cost(micros):
    return pl.CostEstimate(flops=int(micros * COST), bytes_accessed=0, transcendentals=0)


def params(mib, **more):
    return pltpu.CompilerParams(vmem_limit_bytes=mib * 1024 * 1024, **more)


def whiten(meta_ref, length_ref, gain_ref, log_ref, slots, pair, held, gram_ref, across_ref, square_ref):
    size, width = held.shape
    slots = [(ref, n) for ref in slots for n in range(ref.shape[0])]
    tile_count = len(slots)
    pair_rows = size // tile_count
    shift = pair_rows.bit_length() - 1
    at = pair + meta_ref[tile_count]
    length = length_ref[at]

    def epoch(shape, axis):
        index = lax.broadcasted_iota(jnp.int32, shape, axis)
        return jnp.bitwise_and(index, pair_rows - 1) * tile_count + jnp.right_shift(index, shift)

    epoch_row, epoch_col = epoch((size, 1), 0), epoch((1, size), 1)
    first_row = jnp.where(epoch_row < length, 1, 0)
    first_col = jnp.where(epoch_col < length, 1, 0)
    gain = jnp.where(epoch_row < length, gain_ref[2 * at], gain_ref[2 * at + 1])
    log_ma = jnp.where(epoch_row < length, log_ref[2 * at], log_ref[2 * at + 1])
    spacing = epoch_row - epoch_col
    lag = jnp.maximum(spacing - 1, 0)
    size_of = gain * jnp.exp(lag.astype(jnp.float32) * log_ma)
    decayed = jnp.where(jnp.bitwise_and(lag, 1) == 1, size_of, -size_of)
    entry = jnp.where(spacing == 0, jnp.float32(1.0), decayed)
    allowed = (first_row == first_col) & (spacing >= 0)
    whitener = jnp.where(allowed, entry, jnp.float32(0.0)).astype(jnp.bfloat16)

    for n, (ref, shard) in enumerate(slots):
        place = pl.ds(pl.multiple_of(meta_ref[n] * pair_rows, pair_rows), pair_rows)
        source = pl.ds(pl.multiple_of(pair * pair_rows, pair_rows), pair_rows)
        held[place, :] = ref[shard, source].astype(jnp.float32)
    rows = held[...]
    obs = rows.astype(jnp.bfloat16)
    lane = lax.broadcasted_iota(jnp.int32, (size, width), 1)
    in_first = jnp.where(lane < width // 2, 1, 0)
    rows = jnp.where(in_first == 1, rows, pltpu.roll(rows, width // 2, axis=1))
    rows = jnp.where(in_first == first_row, rows, 0.0).astype(jnp.bfloat16)
    white = jnp.dot(whitener, rows, preferred_element_type=jnp.float32)
    eye = lax.broadcasted_iota(jnp.int32, (width, width), 0) == lax.broadcasted_iota(
        jnp.int32, (width, width), 1
    )
    gram = lax.dot_general(
        white, white, ROWS_ACROSS, precision=HIGHEST, preferred_element_type=jnp.float32
    ) + jnp.where(eye, 1.0, 0.0)
    second = lax.broadcasted_iota(jnp.int32, (width // 2, width), 1) >= width // 2
    gram_ref[pair] = jnp.where(second, gram[width // 2 :], gram[: width // 2])
    high = white.astype(jnp.bfloat16)
    rest = white - high.astype(jnp.float32)
    middle = rest.astype(jnp.bfloat16)
    low = (rest - middle.astype(jnp.float32)).astype(jnp.bfloat16)
    across_ref[pair] = sum(
        lax.dot_general(part, whitener, ROWS_ACROSS, preferred_element_type=jnp.float32)
        for part in (low, middle, high)
    )
    square_ref[pair] = lax.dot_general(
        whitener, whitener, ROWS_ACROSS, preferred_element_type=jnp.float32
    )
    return obs


def sweep(held):
    pairs, half, size = held.shape
    lane = lax.broadcasted_iota(jnp.int32, (half, size), 1)
    in_half = jnp.bitwise_and(lane, half - 1)
    base = lane - in_half
    at = lax.broadcasted_iota(jnp.int32, (half, size), 0)
    every = range(pairs)

    @pl.loop(0, half)
    def _(k):
        pick = base + k
        here = in_half == k
        rows = [jnp.broadcast_to(held[b, pl.ds(k, 1), :], (8, size)) for b in every]
        wholes = [held[b] for b in every]
        pivots = [jnp.take_along_axis(rows[b], pick[:8], axis=1)[:1] for b in every]
        columns = [jnp.take_along_axis(wholes[b], pick, axis=1) for b in every]
        inverses = [1.0 / pivots[b] for b in every]
        scaled = [rows[b][:1] * inverses[b] for b in every]
        swept = [
            jnp.where(here, columns[b] * inverses[b], wholes[b] - columns[b] * scaled[b]) for b in every
        ]
        for b in every:
            held[b] = jnp.where(at == k, jnp.where(here, -inverses[b], scaled[b]), swept[b])


def finish(across, minus, square, obs, tile_count):
    size = square.shape[0]
    half, width = minus.shape
    second = lax.broadcasted_iota(jnp.int32, (half, width), 1) >= half
    minus = jnp.concatenate([jnp.where(second, 0.0, minus), jnp.where(second, minus, 0.0)], axis=0)
    reduced = jnp.dot(minus, across, precision=HIGHEST, preferred_element_type=jnp.float32)
    whole = square + lax.dot_general(
        across, reduced, ROWS_ACROSS, precision=HIGHEST, preferred_element_type=jnp.float32
    )
    high = whole.astype(jnp.bfloat16)
    rest = whole - high.astype(jnp.float32)
    middle = rest.astype(jnp.bfloat16)
    low = (rest - middle.astype(jnp.float32)).astype(jnp.bfloat16)
    value = sum(
        jnp.dot(part, obs, preferred_element_type=jnp.float32) for part in (low, middle, high)
    )
    value = jnp.broadcast_to(value[:, width // 2 : width // 2 + 1], (size, EXTRA))
    value_high = value.astype(jnp.bfloat16).astype(jnp.float32)
    rest = value - value_high
    value_middle = rest.astype(jnp.bfloat16).astype(jnp.float32)
    value_low = rest - value_middle
    row = lax.broadcasted_iota(jnp.int32, (size, EXTRA), 0)
    lane = lax.broadcasted_iota(jnp.int32, (size, EXTRA), 1)
    shard = jnp.right_shift(row, (size // tile_count).bit_length() - 1)
    parts = jnp.where(lane == shard, value_high, 0.0)
    parts = jnp.where(lane == shard + tile_count, value_middle, parts)
    parts = jnp.where(lane == shard + 2 * tile_count, value_low, parts)
    return high, middle, parts.astype(jnp.bfloat16)


def pair_kernel(meta_ref, length_ref, gain_ref, log_ref, *refs):
    *slots, out_ref, held, gram, across, square, obs, turn = refs
    size = square.shape[1]
    tile_count = sum(ref.shape[0] for ref in slots)
    pair_rows = size // tile_count

    @pl.loop(0, square.shape[0])
    def _(pair):
        obs[pair] = whiten(
            meta_ref, length_ref, gain_ref, log_ref, slots, pair, held, gram, across, square
        )

    sweep(gram)

    @pl.loop(0, square.shape[0])
    def _(pair):
        high, middle, parts = finish(across[pair], gram[pair], square[pair], obs[pair], tile_count)
        turn[:, :size] = high
        turn[:, size : 2 * size] = middle
        turn[:, 2 * size :] = parts
        for n in range(tile_count):
            place = pl.ds(pl.multiple_of(meta_ref[n] * pair_rows, pair_rows), pair_rows)
            out_ref[pair, n * pair_rows : (n + 1) * pair_rows] = turn[place, :]


def pair_matrices(slots, shard, first_pair, arc_of_row, autoreg, movavg, pair_rows):
    tile_count = sum(slot.shape[0] for slot in slots)
    rows, width = slots[0].shape[1:]
    param_count = width // 2
    pair_count = rows // pair_rows
    size = tile_count * pair_rows
    meta = jnp.concatenate([shard, jnp.reshape(first_pair, (1,)).astype(jnp.int32)])
    first = 2 * jnp.arange(autoreg.shape[0] // 2, dtype=jnp.int32)
    lengths = jnp.sum((arc_of_row == first[None, :]).astype(jnp.int32), axis=0)
    return pl.pallas_call(
        pair_kernel,
        in_specs=[SMEM] * 4 + [pl.BlockSpec(memory_space=pltpu.VMEM)] * len(slots),
        out_specs=pl.BlockSpec(memory_space=pltpu.VMEM),
        out_shape=jax.ShapeDtypeStruct((pair_count, size, 2 * size + EXTRA), jnp.bfloat16),
        scratch_shapes=[
            pltpu.VMEM((size, width), jnp.float32),
            pltpu.VMEM((pair_count, param_count, width), jnp.float32),
            pltpu.VMEM((pair_count, width, size), jnp.float32),
            pltpu.VMEM((pair_count, size, size), jnp.float32),
            pltpu.VMEM((pair_count, size, width), jnp.bfloat16),
            pltpu.VMEM((size, 2 * size + EXTRA), jnp.bfloat16),
        ],
        compiler_params=params(58),
        cost_estimate=cost(SMALL * 2),
        name="pair_matrices",
    )(meta, lengths, autoreg + movavg, jnp.log(movavg), *slots)


def pack_kernel(count, width, meta_ref, *refs):
    slots, out, held, sems = refs[:count], refs[count], refs[count + 1], refs[count + 2]
    start = pl.multiple_of(meta_ref[1], 128)

    @pl.when(meta_ref[0] == 1)
    def _():
        into, back, at = [], [], 0
        for n, slot in enumerate(slots):
            here = pl.ds(at, slot.shape[0])
            columns = slot.at[:, pl.ds(start, width)]
            into.append(pltpu.make_async_copy(columns, held.at[here], sems.at[0, n]))
            back.append(pltpu.make_async_copy(held.at[here], out.at[here], sems.at[1, n]))
            at += slot.shape[0]
        for copy in into:
            copy.start()
        for first, second in zip(into, back):
            first.wait()
            second.start()
        for copy in back:
            copy.wait()


def pack(meta, slots, width):
    rows = sum(slot.shape[0] for slot in slots)
    return pl.pallas_call(
        functools.partial(pack_kernel, len(slots), width),
        in_specs=[SMEM] + [HBM] * len(slots),
        out_specs=HBM,
        out_shape=jax.ShapeDtypeStruct((rows, width), slots[0].dtype),
        scratch_shapes=[
            pltpu.VMEM((rows, width), slots[0].dtype),
            pltpu.SemaphoreType.DMA((2, len(slots))),
        ],
        cost_estimate=cost(SMALL * 2),
        name="pack",
    )(meta, *slots)


def middle_rows_kernel(count, scale, meta_ref, *refs):
    mids, slots, (out, rhs, panel, held, sems, middle, extra) = refs[:2], refs[2 : 2 + count], refs[2 + count :]
    pair_rows = slots[0].shape[0]
    size = count * pair_rows
    pair, pairs = pl.program_id(0), held.shape[0]
    core = meta_ref[count]

    def fetch(which, kind):
        source = mids[kind].at[which % (pairs // 2)]
        return pltpu.make_async_copy(source, held.at[which], sems.at[which])

    @pl.when(pair == 0)
    def _():
        for mine in range(2):

            @pl.when(core == mine)
            def _(mine=mine):
                for which in range(pairs):
                    fetch(which, int(which // (pairs // 2) != mine)).start()

    for n, slot in enumerate(slots):
        panel[n * pair_rows : (n + 1) * pair_rows, :] = slot[...]
    fetch(pair, 0).wait()
    product = lax.dot_general(
        held[pair], panel[...], ROWS_ACROSS, preferred_element_type=jnp.float32
    )
    middle[...] = (product[:size] + product[size : 2 * size]).astype(jnp.bfloat16)
    for n in range(count):
        place = pl.ds(pl.multiple_of(meta_ref[n] * pair_rows, pair_rows), pair_rows)
        out[n] = middle[place, :]

    @pl.when(pair == 0)
    def _():
        extra[...] = product[2 * size :]

    @pl.when(pair > 0)
    def _():
        extra[...] += product[2 * size :]

    @pl.when(pair == pairs - 1)
    def _():
        rhs[...] = jnp.sum(extra[...], axis=0, keepdims=True) * scale


def middle_rows(meta, mids, slots, pair_rows, scale):
    rows, width = slots[0].shape
    pair_count, size, columns = rows // pair_rows, mids[0].shape[1], mids[0].shape[2]
    count = len(slots)
    return pl.pallas_call(
        functools.partial(middle_rows_kernel, count, scale),
        grid=(pair_count,),
        in_specs=[SMEM] + [HBM] * 2 + [pl.BlockSpec((pair_rows, width), lambda b: (b, 0))] * count,
        out_specs=[
            pl.BlockSpec((count, pair_rows, width), lambda b: (0, b, 0)),
            pl.BlockSpec((1, width), lambda b: (0, 0)),
        ],
        out_shape=[
            jax.ShapeDtypeStruct((count, rows, width), jnp.bfloat16),
            jax.ShapeDtypeStruct((1, width), jnp.float32),
        ],
        scratch_shapes=[
            pltpu.VMEM((size, width), jnp.bfloat16),
            pltpu.VMEM((pair_count, size, columns), jnp.bfloat16),
            pltpu.SemaphoreType.DMA((pair_count,)),
            pltpu.VMEM((size, width), jnp.bfloat16),
            pltpu.VMEM((EXTRA, width), jnp.float32),
        ],
        compiler_params=params(56),
        cost_estimate=cost(ROWS),
        name="middle_rows",
    )(meta, *mids, *slots)


def collect_kernel(slot_places, over_places, slot_count, meta_ref, *refs):
    slots, overs, (out, held, sems) = refs[:slot_count], refs[slot_count:-3], refs[-3:]
    width = held.shape[1]
    rows = held.shape[0] // len(slot_places)
    start = pl.multiple_of(meta_ref[2], 128)

    def copies(near):
        found = []
        for n in range(len(slot_places)):
            which, at = slot_places[n] if near else over_places[n]
            ref = slots[which].at[pl.ds(at, rows), pl.ds(start, width)] if near else overs[which].at[pl.ds(at, rows)]
            found.append(pltpu.make_async_copy(ref, held.at[pl.ds(n * rows, rows)], sems.at[n]))
        return found

    for near in (True, False):

        @pl.when((meta_ref[0] == 1) & (meta_ref[1] == int(near)))
        def _(near=near):
            for copy in copies(near):
                copy.start()
            for n, copy in enumerate(copies(near)):
                copy.wait()
                out[:, n * rows : (n + 1) * rows] = held[n * rows : (n + 1) * rows, :].T


def collect(meta, slots, slot_places, overs, over_places, rows, width):
    total = rows * len(slot_places)
    return pl.pallas_call(
        functools.partial(collect_kernel, tuple(slot_places), tuple(over_places), len(slots)),
        in_specs=[SMEM] + [HBM] * (len(slots) + len(overs)),
        out_specs=pl.BlockSpec(memory_space=pltpu.VMEM),
        out_shape=jax.ShapeDtypeStruct((width, total), jnp.bfloat16),
        scratch_shapes=[
            pltpu.VMEM((total, width), jnp.bfloat16),
            pltpu.SemaphoreType.DMA((len(slot_places),)),
        ],
        compiler_params=params(24),
        cost_estimate=cost(SMALL * 2),
        name="collect",
    )(meta, *slots, *overs)


def tile_kernel(block_columns, scale, meta_ref, *refs):
    blocks, (*middles, out, block, sems) = refs[:4], refs[4:]
    step = middles[0].shape[2]

    def copies(kind):
        found, at = [], 0
        for n, ref in enumerate(blocks[2 * kind : 2 * kind + 2]):
            count = ref.shape[1]
            found.append(pltpu.make_async_copy(ref, block.at[:, pl.ds(at, count)], sems.at[n]))
            at += count
        return found

    @pl.when(pl.program_id(0) == 0)
    def _():
        for kind in range(2):

            @pl.when(meta_ref[0] != kind)
            def _(kind=kind):
                for copy in copies(kind):
                    copy.start()

        for copy in copies(0):
            copy.wait()

    middle = jnp.concatenate([one[...].reshape(-1, step) for one in middles], axis=0)
    offset = pl.multiple_of(meta_ref[3], 64)
    out[...] = (
        jnp.dot(block[pl.ds(offset, block_columns), :], middle, preferred_element_type=jnp.float32)
        * scale
    )


def tile(meta, middles, blocks, block_columns, scale, step):
    count, rows, width = middles[0].shape
    payload = blocks[0].shape[0]
    total = count * rows * len(middles)
    return pl.pallas_call(
        functools.partial(tile_kernel, block_columns, scale),
        grid=(pl.cdiv(width, step),),
        in_specs=[SMEM]
        + [HBM] * 4
        + [pl.BlockSpec((count, rows, step), lambda j: (0, 0, j))] * len(middles),
        out_specs=pl.BlockSpec((block_columns, step), lambda j: (0, j)),
        out_shape=jax.ShapeDtypeStruct((block_columns, width), jnp.float32),
        scratch_shapes=[pltpu.VMEM((payload, total), jnp.bfloat16), pltpu.SemaphoreType.DMA((2,))],
        compiler_params=params(48),
        cost_estimate=cost(12),
        name="tile",
    )(meta, *blocks, *middles)


def tie(value, *others):
    return lax.optimization_barrier((value, *others))[0]


def block_body(design, partials, observed, arc_of_row, autoreg, movavg):
    tile_count, panel_count = lax.axis_size("tm"), lax.axis_size("panel")
    rows_dev, width = design.shape
    block_columns = width * panel_count // tile_count
    payload = pl.cdiv(block_columns, 128) * 128
    pair_rows = 2 * rows_dev // tile_count
    scale = 1.0 / (rows_dev * tile_count)
    t, p = lax.axis_index("tm"), lax.axis_index("panel")
    z, x, y, core = t // 2, t % 2, p // 2, p % 2
    near, same_core = y == z // 2, core == z % 2

    def along_z(value, turn):
        pairs = [(2 * s + i, 2 * d + i) for s, d in SEND_Z[turn] for i in range(2)]
        return lax.ppermute(value, "tm", pairs)

    def across_x(value):
        return lax.ppermute(value, "tm", [(s, s ^ 1) for s in range(tile_count)])

    def hop(value, go):
        pairs = []
        for s in range(tile_count * panel_count):
            sz, sy, sc = s // 8, s // 2 % 2, s % 2
            to = go(sy == sz // 2, sc == sz % 2)
            if to is not None:
                pairs.append((s, s - s % 4 + (sy ^ to[0]) * 2 + (sc ^ to[1])))
        return lax.ppermute(value, AXES, pairs)

    line = [z] + [lax.rem((turn + 2) * z + turn + 1, 5) for turn in range(3)]
    shard = jnp.stack([2 * s + i for s in line for i in (x, 1 - x)]).astype(jnp.int32)

    half = rows_dev // 2
    pairs = half // pair_rows
    sent = jnp.concatenate([partials, jnp.broadcast_to(observed[:, None], partials.shape)], axis=1)
    sent = jnp.where(core == 0, sent[:half], sent[half:])
    both = jnp.stack([sent, across_x(sent)])
    sent_z = [both] + [along_z(both, turn) for turn in (0, 1, 3)]
    z1 = along_z(design, 0)
    x0 = across_x(tie(design, both))
    sent_z[0] = tie(sent_z[0], z1, x0)
    mid = pair_matrices(sent_z, shard, core * pairs, arc_of_row, autoreg, movavg, pair_rows)

    start = x * (width - payload)
    sends = (near & same_core).astype(jnp.int32)

    def picked(start, *slots):
        return pack(jnp.stack([sends, start]), slots, payload)

    def over(value):
        return hop(value, lambda near, same: (1, 0) if near and same else None)

    def beside(value):
        return hop(value, lambda near, same: (0, 1) if same else None)

    z2 = along_z(tie(design, z1, x0, *sent_z), 1)
    x1 = across_x(tie(z1, x0))
    z3 = along_z(tie(z1, z2, x1, mid), 2)
    x2 = across_x(tie(z2, x1))
    picked_1 = picked(start, design, x0, z1, x1, tie(z2, mid))
    mids = (mid, hop(tie(mid, z2), lambda near, same: (0, 1)))
    slots_meta = jnp.concatenate([shard, core[None]])
    x3 = across_x(tie(z3, x2, picked_1, mids[1]))
    picked_2 = picked(start, x2, z3)
    picked_3 = picked((1 - x) * (width - payload), z3)
    over_1, over_2 = over(picked_1), over(picked_2)
    over_3 = across_x(tie(over(picked_3), x3))

    block_meta = jnp.stack(
        [same_core.astype(jnp.int32), near.astype(jnp.int32), start, x * (payload - block_columns)]
    )
    early = collect(
        block_meta,
        (design, x0, z1, x1, z2),
        [(n, 0) for n in range(5)],
        (over_1,),
        [(0, n * rows_dev) for n in range(5)],
        rows_dev,
        payload,
    )
    slots = (design, x0, z1, x1, z2, x2, z3, tie(x3, early))
    middle, rhs = middle_rows(slots_meta, mids, slots, pair_rows, scale)
    late = collect(
        block_meta, (x2, z3, tie(x3, rhs)), [(0, 0), (1, 0), (2, 0)],
        (over_2, over_3), [(0, 0), (0, rows_dev), (1, 0)], rows_dev, payload,
    )
    blocks = (early, late, beside(early), beside(late))
    normal = tile(block_meta, (middle,), blocks, block_columns, scale, 512)
    return normal, rhs[0]


def line_body(design, partials, observed, arc_of_row, autoreg, movavg):
    tile_count = lax.axis_size("tm")
    rows_dev, width = design.shape
    pair_rows = 2 * rows_dev // tile_count
    pair_count = rows_dev // pair_rows
    size = tile_count * pair_rows
    scale = 1.0 / (rows_dev * tile_count)
    sent = jnp.concatenate([partials, jnp.broadcast_to(observed[:, None], partials.shape)], axis=1)
    sent = lax.all_gather(sent, "tm", axis=0, tiled=False)
    shard = jnp.arange(tile_count, dtype=jnp.int32)
    mids = pair_matrices([sent], shard, 0, arc_of_row, autoreg, movavg, pair_rows)
    panel = lax.all_gather(design, "tm", axis=0, tiled=False)
    whole_rows = lax.all_gather(design, "panel", axis=1, tiled=True)
    block = lax.all_to_all(whole_rows, "tm", split_axis=1, concat_axis=0, tiled=True)
    block = block.reshape(tile_count, rows_dev, -1)

    def one_pair(sums, pair):
        def rows_of(values):
            here = lax.dynamic_slice_in_dim(values, pair * pair_rows, pair_rows, 1)
            return here.reshape(size, values.shape[2])

        product = lax.dot_general(
            mids[pair], rows_of(panel), ROWS_ACROSS, preferred_element_type=jnp.float32
        )
        middle = (product[:size] + product[size : 2 * size]).astype(jnp.bfloat16)
        here = lax.dot_general(
            rows_of(block), middle, ROWS_ACROSS, preferred_element_type=jnp.float32
        )
        return (sums[0] + here, sums[1] + jnp.sum(product[2 * size :], axis=0)), None

    start = (jnp.zeros((block.shape[2], width), jnp.float32), jnp.zeros((width,), jnp.float32))
    (normal, right_hand), _ = lax.scan(one_pair, start, jnp.arange(pair_count))
    return normal * scale, right_hand * scale


def solution(mesh):
    in_specs = (P("tm", "panel"), P("tm", None), P("tm"), P(), P(), P())
    out_specs = (P("tm", "panel"), P("panel"))
    body = block_body if (mesh.shape["tm"], mesh.shape["panel"]) == (8, 4) else line_body
    return jax.shard_map(body, mesh=mesh, in_specs=in_specs, out_specs=out_specs, check_vma=False)
```

```python
import functools

import jax
import jax.numpy as jnp
from jax import lax
from jax.experimental import pallas as pl
from jax.experimental.pallas import tpu as pltpu
from jax.sharding import PartitionSpec as P

AXES = ("tm", "panel")
HIGHEST = lax.Precision.HIGHEST
ROWS_ACROSS = (((0,), (0,)), ((), ()))
EXTRA = 16
HBM = pl.BlockSpec(memory_space=pl.ANY)
SMEM = pl.BlockSpec(memory_space=pltpu.SMEM)
SEND_Z = (((1, 0), (3, 1), (0, 2), (2, 3)), ((2, 0), (0, 1), (3, 2), (1, 3)), ((1, 0), (3, 1), (0, 2), (2, 3)), ((3, 0), (2, 1), (1, 2), (0, 3)))


COST = 1e9
SMALL = 0.5
ROWS = 12


def cost(micros):
    return pl.CostEstimate(flops=int(micros * COST), bytes_accessed=0, transcendentals=0)


def params(mib, **more):
    return pltpu.CompilerParams(vmem_limit_bytes=mib * 1024 * 1024, **more)


def whiten(meta_ref, length_ref, gain_ref, log_ref, slots, pair, held, gram_ref, across_ref, square_ref):
    size, width = held.shape
    slots = [(ref, n) for ref in slots for n in range(ref.shape[0])]
    tile_count = len(slots)
    pair_rows = size // tile_count
    shift = pair_rows.bit_length() - 1
    at = pair + meta_ref[tile_count]
    length = length_ref[at]

    def epoch(shape, axis):
        index = lax.broadcasted_iota(jnp.int32, shape, axis)
        return jnp.bitwise_and(index, pair_rows - 1) * tile_count + jnp.right_shift(index, shift)

    epoch_row, epoch_col = epoch((size, 1), 0), epoch((1, size), 1)
    first_row = jnp.where(epoch_row < length, 1, 0)
    first_col = jnp.where(epoch_col < length, 1, 0)
    gain = jnp.where(epoch_row < length, gain_ref[2 * at], gain_ref[2 * at + 1])
    log_ma = jnp.where(epoch_row < length, log_ref[2 * at], log_ref[2 * at + 1])
    spacing = epoch_row - epoch_col
    lag = jnp.maximum(spacing - 1, 0)
    size_of = gain * jnp.exp(lag.astype(jnp.float32) * log_ma)
    decayed = jnp.where(jnp.bitwise_and(lag, 1) == 1, size_of, -size_of)
    entry = jnp.where(spacing == 0, jnp.float32(1.0), decayed)
    allowed = (first_row == first_col) & (spacing >= 0)
    whitener = jnp.where(allowed, entry, jnp.float32(0.0)).astype(jnp.bfloat16)

    for n, (ref, shard) in enumerate(slots):
        place = pl.ds(pl.multiple_of(meta_ref[n] * pair_rows, pair_rows), pair_rows)
        source = pl.ds(pl.multiple_of(pair * pair_rows, pair_rows), pair_rows)
        held[place, :] = ref[shard, source].astype(jnp.float32)
    rows = held[...]
    obs = rows.T[width // 2 : width // 2 + EXTRA].astype(jnp.bfloat16)
    lane = lax.broadcasted_iota(jnp.int32, (size, width), 1)
    in_first = jnp.where(lane < width // 2, 1, 0)
    rows = jnp.where(in_first == 1, rows, pltpu.roll(rows, width // 2, axis=1))
    rows = jnp.where(in_first == first_row, rows, 0.0).astype(jnp.bfloat16)
    white = jnp.dot(whitener, rows, preferred_element_type=jnp.float32)
    eye = lax.broadcasted_iota(jnp.int32, (width, width), 0) == lax.broadcasted_iota(
        jnp.int32, (width, width), 1
    )
    gram = lax.dot_general(
        white, white, ROWS_ACROSS, precision=HIGHEST, preferred_element_type=jnp.float32
    ) + jnp.where(eye, 1.0, 0.0)
    second = lax.broadcasted_iota(jnp.int32, (width // 2, width), 1) >= width // 2
    gram_ref[pair] = jnp.where(second, gram[width // 2 :], gram[: width // 2])
    high = white.astype(jnp.bfloat16)
    rest = white - high.astype(jnp.float32)
    middle = rest.astype(jnp.bfloat16)
    low = (rest - middle.astype(jnp.float32)).astype(jnp.bfloat16)
    across_ref[pair] = sum(
        lax.dot_general(part, whitener, ROWS_ACROSS, preferred_element_type=jnp.float32)
        for part in (low, middle, high)
    )
    square_ref[pair] = lax.dot_general(
        whitener, whitener, ROWS_ACROSS, preferred_element_type=jnp.float32
    )
    return obs


def sweep(held):
    pairs, half, size = held.shape
    lane = lax.broadcasted_iota(jnp.int32, (half, size), 1)
    in_half = jnp.bitwise_and(lane, half - 1)
    base = lane - in_half
    at = lax.broadcasted_iota(jnp.int32, (half, size), 0)
    every = range(pairs)

    @pl.loop(0, half)
    def _(k):
        pick = base + k
        here = in_half == k
        rows = [jnp.broadcast_to(held[b, pl.ds(k, 1), :], (8, size)) for b in every]
        wholes = [held[b] for b in every]
        pivots = [jnp.take_along_axis(rows[b], pick[:8], axis=1)[:1] for b in every]
        columns = [jnp.take_along_axis(wholes[b], pick, axis=1) for b in every]
        inverses = [1.0 / pivots[b] for b in every]
        scaled = [rows[b][:1] * inverses[b] for b in every]
        swept = [
            jnp.where(here, columns[b] * inverses[b], wholes[b] - columns[b] * scaled[b]) for b in every
        ]
        for b in every:
            held[b] = jnp.where(at == k, jnp.where(here, -inverses[b], scaled[b]), swept[b])


def finish(across, minus, square, obs):
    size = square.shape[0]
    half, width = minus.shape
    second = lax.broadcasted_iota(jnp.int32, (half, width), 1) >= half
    minus = jnp.concatenate([jnp.where(second, 0.0, minus), jnp.where(second, minus, 0.0)], axis=0)
    reduced = jnp.dot(minus, across, precision=HIGHEST, preferred_element_type=jnp.float32)
    whole = square + lax.dot_general(
        across, reduced, ROWS_ACROSS, precision=HIGHEST, preferred_element_type=jnp.float32
    )
    high = whole.astype(jnp.bfloat16)
    rest = whole - high.astype(jnp.float32)
    middle = rest.astype(jnp.bfloat16)
    low = (rest - middle.astype(jnp.float32)).astype(jnp.bfloat16)
    value = sum(
        jnp.dot(obs, part, preferred_element_type=jnp.float32) for part in (low, middle, high)
    )
    value_high = value.astype(jnp.bfloat16).astype(jnp.float32)
    rest = value - value_high
    value_middle = rest.astype(jnp.bfloat16).astype(jnp.float32)
    value_low = rest - value_middle
    at = lax.broadcasted_iota(jnp.int32, (EXTRA, size), 0)
    parts = jnp.where(at == 0, value_high, 0.0)
    parts = jnp.where(at == 1, value_middle, parts)
    parts = jnp.where(at == 2, value_low, parts)
    return high, middle, parts.astype(jnp.bfloat16)


def pair_kernel(meta_ref, length_ref, gain_ref, log_ref, *refs):
    *slots, out_ref, held, gram, across, square, obs, turn = refs
    size = square.shape[1]
    tile_count = sum(ref.shape[0] for ref in slots)
    pair_rows = size // tile_count

    @pl.loop(0, square.shape[0])
    def _(pair):
        obs[pair] = whiten(
            meta_ref, length_ref, gain_ref, log_ref, slots, pair, held, gram, across, square
        )

    sweep(gram)

    @pl.loop(0, square.shape[0])
    def _(pair):
        high, middle, parts = finish(across[pair], gram[pair], square[pair], obs[pair])
        out_ref[pair, 2 * size :] = parts
        for first, part in ((0, high), (size, middle)):
            turn[...] = part
            for n in range(tile_count):
                place = pl.ds(pl.multiple_of(meta_ref[n] * pair_rows, pair_rows), pair_rows)
                out_ref[pair, first + n * pair_rows : first + (n + 1) * pair_rows] = turn[place, :]


def pair_matrices(slots, shard, first_pair, arc_of_row, autoreg, movavg, pair_rows):
    tile_count = sum(slot.shape[0] for slot in slots)
    rows, width = slots[0].shape[1:]
    param_count = width // 2
    pair_count = rows // pair_rows
    size = tile_count * pair_rows
    meta = jnp.concatenate([shard, jnp.reshape(first_pair, (1,)).astype(jnp.int32)])
    first = 2 * jnp.arange(autoreg.shape[0] // 2, dtype=jnp.int32)
    lengths = jnp.sum((arc_of_row == first[None, :]).astype(jnp.int32), axis=0)
    return pl.pallas_call(
        pair_kernel,
        in_specs=[SMEM] * 4 + [pl.BlockSpec(memory_space=pltpu.VMEM)] * len(slots),
        out_specs=pl.BlockSpec(memory_space=pltpu.VMEM),
        out_shape=jax.ShapeDtypeStruct((pair_count, 2 * size + EXTRA, size), jnp.bfloat16),
        scratch_shapes=[
            pltpu.VMEM((size, width), jnp.float32),
            pltpu.VMEM((pair_count, param_count, width), jnp.float32),
            pltpu.VMEM((pair_count, width, size), jnp.float32),
            pltpu.VMEM((pair_count, size, size), jnp.float32),
            pltpu.VMEM((pair_count, EXTRA, size), jnp.bfloat16),
            pltpu.VMEM((size, size), jnp.bfloat16),
        ],
        compiler_params=params(58),
        cost_estimate=cost(SMALL * 2),
        name="pair_matrices",
    )(meta, lengths, autoreg + movavg, jnp.log(movavg), *slots)


def pack_kernel(count, width, meta_ref, *refs):
    slots, out, held, sems = refs[:count], refs[count], refs[count + 1], refs[count + 2]
    start = pl.multiple_of(meta_ref[1], 128)

    @pl.when(meta_ref[0] == 1)
    def _():
        into, back, at = [], [], 0
        for n, slot in enumerate(slots):
            here = pl.ds(at, slot.shape[0])
            columns = slot.at[:, pl.ds(start, width)]
            into.append(pltpu.make_async_copy(columns, held.at[here], sems.at[0, n]))
            back.append(pltpu.make_async_copy(held.at[here], out.at[here], sems.at[1, n]))
            at += slot.shape[0]
        for copy in into:
            copy.start()
        for first, second in zip(into, back):
            first.wait()
            second.start()
        for copy in back:
            copy.wait()


def pack(meta, slots, width):
    rows = sum(slot.shape[0] for slot in slots)
    return pl.pallas_call(
        functools.partial(pack_kernel, len(slots), width),
        in_specs=[SMEM] + [HBM] * len(slots),
        out_specs=HBM,
        out_shape=jax.ShapeDtypeStruct((rows, width), slots[0].dtype),
        scratch_shapes=[
            pltpu.VMEM((rows, width), slots[0].dtype),
            pltpu.SemaphoreType.DMA((2, len(slots))),
        ],
        cost_estimate=cost(SMALL * 2),
        name="pack",
    )(meta, *slots)


def middle_rows_kernel(count, scale, step, meta_ref, *refs):
    mids, slots, (out, rhs, panel, held, sems) = refs[:2], refs[2 : 2 + count], refs[2 + count :]
    pair_rows, width = slots[0].shape
    size = count * pair_rows
    pair, pairs = pl.program_id(0), held.shape[0]
    core = meta_ref[count]

    def fetch(which, kind):
        source = mids[kind].at[which % (pairs // 2)]
        return pltpu.make_async_copy(source, held.at[which], sems.at[which])

    @pl.when(pair == 0)
    def _():
        rhs[...] = jnp.zeros_like(rhs)
        for mine in range(2):

            @pl.when(core == mine)
            def _(mine=mine):
                for which in range(pairs):
                    fetch(which, int(which // (pairs // 2) != mine)).start()

    for n, slot in enumerate(slots):
        place = pl.ds(pl.multiple_of(meta_ref[n] * pair_rows, pair_rows), pair_rows)
        panel[place, :] = slot[...]
    fetch(pair, 0).wait()
    for at in range(0, width, step):
        here = slice(at, min(at + step, width))
        product = jnp.dot(held[pair], panel[:, here], preferred_element_type=jnp.float32)
        middle = (product[:size] + product[size : 2 * size]).astype(jnp.bfloat16)
        for n in range(count):
            out[n, :, here] = middle[n * pair_rows : (n + 1) * pair_rows]
        rhs[:, here] += jnp.sum(product[2 * size :], axis=0, keepdims=True) * scale


def middle_rows(meta, mids, slots, pair_rows, scale, step):
    rows, width = slots[0].shape
    pair_count, size, columns = rows // pair_rows, mids[0].shape[2], mids[0].shape[1]
    count = len(slots)
    return pl.pallas_call(
        functools.partial(middle_rows_kernel, count, scale, step),
        grid=(pair_count,),
        in_specs=[SMEM] + [HBM] * 2 + [pl.BlockSpec((pair_rows, width), lambda b: (b, 0))] * count,
        out_specs=[
            pl.BlockSpec((count, pair_rows, width), lambda b: (0, b, 0)),
            pl.BlockSpec((1, width), lambda b: (0, 0)),
        ],
        out_shape=[
            jax.ShapeDtypeStruct((count, rows, width), jnp.bfloat16),
            jax.ShapeDtypeStruct((1, width), jnp.float32),
        ],
        scratch_shapes=[
            pltpu.VMEM((size, width), jnp.bfloat16),
            pltpu.VMEM((pair_count, columns, size), jnp.bfloat16),
            pltpu.SemaphoreType.DMA((pair_count,)),
        ],
        compiler_params=params(48),
        cost_estimate=cost(ROWS),
        name="middle_rows",
    )(meta, *mids, *slots)


def collect_kernel(slot_places, over_places, slot_count, meta_ref, *refs):
    slots, overs, (out, held, turned, sems) = refs[:slot_count], refs[slot_count:-4], refs[-4:]
    offset = pl.multiple_of(meta_ref[3], 64)
    width = held.shape[1]
    rows = held.shape[0] // len(slot_places)
    start = pl.multiple_of(meta_ref[2], 128)

    def copies(near):
        found = []
        for n in range(len(slot_places)):
            which, at = slot_places[n] if near else over_places[n]
            ref = slots[which].at[pl.ds(at, rows), pl.ds(start, width)] if near else overs[which].at[pl.ds(at, rows)]
            found.append(pltpu.make_async_copy(ref, held.at[pl.ds(n * rows, rows)], sems.at[n]))
        return found

    for near in (True, False):

        @pl.when((meta_ref[0] == 1) & (meta_ref[1] == int(near)))
        def _(near=near):
            for copy in copies(near):
                copy.start()
            for n, copy in enumerate(copies(near)):
                copy.wait()
                turned[...] = held[n * rows : (n + 1) * rows, :].T
                out[:, n * rows : (n + 1) * rows] = turned[pl.ds(offset, out.shape[0]), :]


def collect(meta, slots, slot_places, overs, over_places, rows, width, block_columns):
    total = rows * len(slot_places)
    return pl.pallas_call(
        functools.partial(collect_kernel, tuple(slot_places), tuple(over_places), len(slots)),
        in_specs=[SMEM] + [HBM] * (len(slots) + len(overs)),
        out_specs=pl.BlockSpec(memory_space=pltpu.VMEM),
        out_shape=jax.ShapeDtypeStruct((block_columns, total), jnp.bfloat16),
        scratch_shapes=[
            pltpu.VMEM((total, width), jnp.bfloat16),
            pltpu.VMEM((width, rows), jnp.bfloat16),
            pltpu.SemaphoreType.DMA((len(slot_places),)),
        ],
        compiler_params=params(24),
        cost_estimate=cost(SMALL * 2),
        name="collect",
    )(meta, *slots, *overs)


def tile_kernel(scale, meta_ref, *refs):
    blocks, (middle_ref, out, block, sems) = refs[:4], refs[4:]

    def copies(kind):
        found, at = [], 0
        for n, ref in enumerate(blocks[2 * kind : 2 * kind + 2]):
            count = ref.shape[1]
            found.append(pltpu.make_async_copy(ref, block.at[:, pl.ds(at, count)], sems.at[n]))
            at += count
        return found

    @pl.when(pl.program_id(0) == 0)
    def _():
        for kind in range(2):

            @pl.when(meta_ref[0] != kind)
            def _(kind=kind):
                for copy in copies(kind):
                    copy.start()

        for copy in copies(0):
            copy.wait()

    middle = middle_ref[...].reshape(-1, middle_ref.shape[2])
    out[...] = jnp.dot(block[...], middle, preferred_element_type=jnp.float32) * scale


def tile(meta, middle, blocks, scale, step):
    count, rows, width = middle.shape
    block_columns = blocks[0].shape[0]
    return pl.pallas_call(
        functools.partial(tile_kernel, scale),
        grid=(pl.cdiv(width, step),),
        in_specs=[SMEM] + [HBM] * 4 + [pl.BlockSpec((count, rows, step), lambda j: (0, 0, j))],
        out_specs=pl.BlockSpec((block_columns, step), lambda j: (0, j)),
        out_shape=jax.ShapeDtypeStruct((block_columns, width), jnp.float32),
        scratch_shapes=[
            pltpu.VMEM((block_columns, count * rows), jnp.bfloat16),
            pltpu.SemaphoreType.DMA((2,)),
        ],
        compiler_params=params(48),
        cost_estimate=cost(12),
        name="tile",
    )(meta, *blocks, middle)


def tie(value, *others):
    return lax.optimization_barrier((value, *others))[0]


def block_body(design, partials, observed, arc_of_row, autoreg, movavg):
    tile_count, panel_count = lax.axis_size("tm"), lax.axis_size("panel")
    rows_dev, width = design.shape
    block_columns = width * panel_count // tile_count
    payload = pl.cdiv(block_columns, 128) * 128
    pair_rows = 2 * rows_dev // tile_count
    scale = 1.0 / (rows_dev * tile_count)
    t, p = lax.axis_index("tm"), lax.axis_index("panel")
    z, x, y, core = t // 2, t % 2, p // 2, p % 2
    near, same_core = y == z // 2, core == z % 2

    def along_z(value, turn):
        pairs = [(2 * s + i, 2 * d + i) for s, d in SEND_Z[turn] for i in range(2)]
        return lax.ppermute(value, "tm", pairs)

    def across_x(value):
        return lax.ppermute(value, "tm", [(s, s ^ 1) for s in range(tile_count)])

    def hop(value, go):
        pairs = []
        for s in range(tile_count * panel_count):
            sz, sy, sc = s // 8, s // 2 % 2, s % 2
            to = go(sy == sz // 2, sc == sz % 2)
            if to is not None:
                pairs.append((s, s - s % 4 + (sy ^ to[0]) * 2 + (sc ^ to[1])))
        return lax.ppermute(value, AXES, pairs)

    line = [z] + [lax.rem((turn + 2) * z + turn + 1, 5) for turn in range(3)]
    shard = jnp.stack([2 * s + i for s in line for i in (x, 1 - x)]).astype(jnp.int32)

    half = rows_dev // 2
    pairs = half // pair_rows
    sent = jnp.concatenate([partials, jnp.broadcast_to(observed[:, None], partials.shape)], axis=1)
    sent = jnp.where(core == 0, sent[:half], sent[half:])
    both = jnp.stack([sent, across_x(sent)])
    sent_z = [both] + [along_z(both, turn) for turn in (0, 1, 3)]
    z1 = along_z(design, 0)
    x0 = across_x(tie(design, both))
    sent_z[0] = tie(sent_z[0], z1, x0)
    mid = pair_matrices(sent_z, shard, core * pairs, arc_of_row, autoreg, movavg, pair_rows)

    start = x * (width - payload)
    sends = (near & same_core).astype(jnp.int32)

    def picked(start, *slots):
        return pack(jnp.stack([sends, start]), slots, payload)

    def over(value):
        return hop(value, lambda near, same: (1, 0) if near and same else None)

    def beside(value):
        return hop(value, lambda near, same: (0, 1) if same else None)

    z2 = along_z(tie(design, z1, x0, *sent_z), 1)
    x1 = across_x(tie(z1, x0))
    z3 = along_z(tie(z1, z2, x1, mid), 2)
    x2 = across_x(tie(z2, x1))
    picked_0 = picked(start, design, x0, tie(z1, z2, mid))
    picked_1 = picked(start, x1, tie(z2, mid))
    mids = (mid, hop(mid, lambda near, same: (0, 1)))
    slots_meta = jnp.concatenate([shard, core[None]])
    x3 = across_x(tie(z3, x2, picked_0, picked_1))
    picked_2 = picked(start, x2, z3)
    picked_3 = picked((1 - x) * (width - payload), z3)
    over_0, over_1, over_2 = over(picked_0), over(picked_1), over(picked_2)
    over_3 = across_x(tie(over(picked_3), x3))

    block_meta = jnp.stack(
        [same_core.astype(jnp.int32), near.astype(jnp.int32), start, x * (payload - block_columns)]
    )
    early = collect(
        block_meta,
        (design, x0, z1, x1, z2),
        [(n, 0) for n in range(5)],
        (over_0, over_1),
        [(n // 3, n % 3 * rows_dev) for n in range(5)],
        rows_dev,
        payload,
        block_columns,
    )
    slots = (design, x0, z1, x1, z2, x2, z3, tie(x3, early))
    middle, rhs = middle_rows(slots_meta, mids, slots, pair_rows, scale, 512)
    late = collect(
        block_meta, (x2, z3, tie(x3, rhs)), [(0, 0), (1, 0), (2, 0)],
        (over_2, over_3), [(0, 0), (0, rows_dev), (1, 0)], rows_dev, payload, block_columns,
    )
    blocks = (early, late, beside(early), beside(late))
    normal = tile(block_meta, middle, blocks, scale, 512)
    return normal, rhs[0]


def line_body(design, partials, observed, arc_of_row, autoreg, movavg):
    tile_count = lax.axis_size("tm")
    rows_dev, width = design.shape
    pair_rows = 2 * rows_dev // tile_count
    pair_count = rows_dev // pair_rows
    size = tile_count * pair_rows
    scale = 1.0 / (rows_dev * tile_count)
    sent = jnp.concatenate([partials, jnp.broadcast_to(observed[:, None], partials.shape)], axis=1)
    sent = lax.all_gather(sent, "tm", axis=0, tiled=False)
    shard = jnp.arange(tile_count, dtype=jnp.int32)
    mids = pair_matrices([sent], shard, 0, arc_of_row, autoreg, movavg, pair_rows)
    panel = lax.all_gather(design, "tm", axis=0, tiled=False)
    whole_rows = lax.all_gather(design, "panel", axis=1, tiled=True)
    block = lax.all_to_all(whole_rows, "tm", split_axis=1, concat_axis=0, tiled=True)
    block = block.reshape(tile_count, rows_dev, -1)

    def one_pair(sums, pair):
        def rows_of(values):
            here = lax.dynamic_slice_in_dim(values, pair * pair_rows, pair_rows, 1)
            return here.reshape(size, values.shape[2])

        product = jnp.dot(mids[pair], rows_of(panel), preferred_element_type=jnp.float32)
        middle = (product[:size] + product[size : 2 * size]).astype(jnp.bfloat16)
        here = lax.dot_general(
            rows_of(block), middle, ROWS_ACROSS, preferred_element_type=jnp.float32
        )
        return (sums[0] + here, sums[1] + jnp.sum(product[2 * size :], axis=0)), None

    start = (jnp.zeros((block.shape[2], width), jnp.float32), jnp.zeros((width,), jnp.float32))
    (normal, right_hand), _ = lax.scan(one_pair, start, jnp.arange(pair_count))
    return normal * scale, right_hand * scale


def solution(mesh):
    in_specs = (P("tm", "panel"), P("tm", None), P("tm"), P(), P(), P())
    out_specs = (P("tm", "panel"), P("panel"))
    body = block_body if (mesh.shape["tm"], mesh.shape["panel"]) == (8, 4) else line_body
    return jax.shard_map(body, mesh=mesh, in_specs=in_specs, out_specs=out_specs, check_vma=False)
```

```python
import functools

import jax
import jax.numpy as jnp
from jax import lax
from jax.experimental import pallas as pl
from jax.experimental.pallas import tpu as pltpu
from jax.sharding import PartitionSpec as P

AXES = ("tm", "panel")
HIGHEST = lax.Precision.HIGHEST
ROWS_ACROSS = (((0,), (0,)), ((), ()))
EXTRA = 16
HBM = pl.BlockSpec(memory_space=pl.ANY)
SMEM = pl.BlockSpec(memory_space=pltpu.SMEM)
SEND_Z = (((1, 0), (3, 1), (0, 2), (2, 3)), ((2, 0), (0, 1), (3, 2), (1, 3)), ((1, 0), (3, 1), (0, 2), (2, 3)), ((3, 0), (2, 1), (1, 2), (0, 3)))


COST = 1e9
SMALL = 0.5
ROWS = 12


def cost(micros):
    return pl.CostEstimate(flops=int(micros * COST), bytes_accessed=0, transcendentals=0)


def params(mib, **more):
    return pltpu.CompilerParams(vmem_limit_bytes=mib * 1024 * 1024, **more)


def whiten(meta_ref, length_ref, gain_ref, log_ref, slots, pair, held, gram_ref, across_ref, square_ref):
    size, width = held.shape
    slots = [(ref, n) for ref in slots for n in range(ref.shape[0])]
    tile_count = len(slots)
    pair_rows = size // tile_count
    shift = pair_rows.bit_length() - 1
    at = pair + meta_ref[tile_count]
    length = length_ref[at]

    def epoch(shape, axis):
        index = lax.broadcasted_iota(jnp.int32, shape, axis)
        return jnp.bitwise_and(index, pair_rows - 1) * tile_count + jnp.right_shift(index, shift)

    epoch_row, epoch_col = epoch((size, 1), 0), epoch((1, size), 1)
    first_row = jnp.where(epoch_row < length, 1, 0)
    first_col = jnp.where(epoch_col < length, 1, 0)
    gain = jnp.where(epoch_row < length, gain_ref[2 * at], gain_ref[2 * at + 1])
    log_ma = jnp.where(epoch_row < length, log_ref[2 * at], log_ref[2 * at + 1])
    spacing = epoch_row - epoch_col
    lag = jnp.maximum(spacing - 1, 0)
    size_of = gain * jnp.exp(lag.astype(jnp.float32) * log_ma)
    decayed = jnp.where(jnp.bitwise_and(lag, 1) == 1, size_of, -size_of)
    entry = jnp.where(spacing == 0, jnp.float32(1.0), decayed)
    allowed = (first_row == first_col) & (spacing >= 0)
    whitener = jnp.where(allowed, entry, jnp.float32(0.0)).astype(jnp.bfloat16)

    for n, (ref, shard) in enumerate(slots):
        place = pl.ds(pl.multiple_of(meta_ref[n] * pair_rows, pair_rows), pair_rows)
        source = pl.ds(pl.multiple_of(pair * pair_rows, pair_rows), pair_rows)
        held[place, :] = ref[shard, source].astype(jnp.float32)
    rows = held[...]
    obs = rows.T[width // 2 : width // 2 + EXTRA].astype(jnp.bfloat16)
    lane = lax.broadcasted_iota(jnp.int32, (size, width), 1)
    in_first = jnp.where(lane < width // 2, 1, 0)
    rows = jnp.where(in_first == 1, rows, pltpu.roll(rows, width // 2, axis=1))
    rows = jnp.where(in_first == first_row, rows, 0.0).astype(jnp.bfloat16)
    white = jnp.dot(whitener, rows, preferred_element_type=jnp.float32)
    eye = lax.broadcasted_iota(jnp.int32, (width, width), 0) == lax.broadcasted_iota(
        jnp.int32, (width, width), 1
    )
    gram = lax.dot_general(
        white, white, ROWS_ACROSS, precision=HIGHEST, preferred_element_type=jnp.float32
    ) + jnp.where(eye, 1.0, 0.0)
    second = lax.broadcasted_iota(jnp.int32, (width // 2, width), 1) >= width // 2
    gram_ref[pair] = jnp.where(second, gram[width // 2 :], gram[: width // 2])
    high = white.astype(jnp.bfloat16)
    rest = white - high.astype(jnp.float32)
    middle = rest.astype(jnp.bfloat16)
    low = (rest - middle.astype(jnp.float32)).astype(jnp.bfloat16)
    across_ref[pair] = sum(
        lax.dot_general(part, whitener, ROWS_ACROSS, preferred_element_type=jnp.float32)
        for part in (low, middle, high)
    )
    square_ref[pair] = lax.dot_general(
        whitener, whitener, ROWS_ACROSS, preferred_element_type=jnp.float32
    )
    return obs


def sweep(held):
    pairs, half, size = held.shape
    lane = lax.broadcasted_iota(jnp.int32, (half, size), 1)
    in_half = jnp.bitwise_and(lane, half - 1)
    base = lane - in_half
    at = lax.broadcasted_iota(jnp.int32, (half, size), 0)
    every = range(pairs)

    @pl.loop(0, half)
    def _(k):
        pick = base + k
        here = in_half == k
        rows = [jnp.broadcast_to(held[b, pl.ds(k, 1), :], (8, size)) for b in every]
        wholes = [held[b] for b in every]
        pivots = [jnp.take_along_axis(rows[b], pick[:8], axis=1)[:1] for b in every]
        columns = [jnp.take_along_axis(wholes[b], pick, axis=1) for b in every]
        inverses = [1.0 / pivots[b] for b in every]
        scaled = [rows[b][:1] * inverses[b] for b in every]
        swept = [
            jnp.where(here, columns[b] * inverses[b], wholes[b] - columns[b] * scaled[b]) for b in every
        ]
        for b in every:
            held[b] = jnp.where(at == k, jnp.where(here, -inverses[b], scaled[b]), swept[b])


def finish(across, minus, square, obs):
    size = square.shape[0]
    half, width = minus.shape
    second = lax.broadcasted_iota(jnp.int32, (half, width), 1) >= half
    minus = jnp.concatenate([jnp.where(second, 0.0, minus), jnp.where(second, minus, 0.0)], axis=0)
    reduced = jnp.dot(minus, across, precision=HIGHEST, preferred_element_type=jnp.float32)
    whole = square + lax.dot_general(
        across, reduced, ROWS_ACROSS, precision=HIGHEST, preferred_element_type=jnp.float32
    )
    high = whole.astype(jnp.bfloat16)
    rest = whole - high.astype(jnp.float32)
    middle = rest.astype(jnp.bfloat16)
    low = (rest - middle.astype(jnp.float32)).astype(jnp.bfloat16)
    value = sum(
        jnp.dot(obs, part, preferred_element_type=jnp.float32) for part in (low, middle, high)
    )
    value_high = value.astype(jnp.bfloat16).astype(jnp.float32)
    rest = value - value_high
    value_middle = rest.astype(jnp.bfloat16).astype(jnp.float32)
    value_low = rest - value_middle
    at = lax.broadcasted_iota(jnp.int32, (EXTRA, size), 0)
    parts = jnp.where(at == 0, value_high, 0.0)
    parts = jnp.where(at == 1, value_middle, parts)
    parts = jnp.where(at == 2, value_low, parts)
    return high, middle, parts.astype(jnp.bfloat16)


def pair_kernel(meta_ref, length_ref, gain_ref, log_ref, *refs):
    *slots, out_ref, held, gram, across, square, obs, turn = refs
    size = square.shape[1]
    tile_count = sum(ref.shape[0] for ref in slots)
    pair_rows = size // tile_count

    @pl.loop(0, square.shape[0])
    def _(pair):
        obs[pair] = whiten(
            meta_ref, length_ref, gain_ref, log_ref, slots, pair, held, gram, across, square
        )

    sweep(gram)

    @pl.loop(0, square.shape[0])
    def _(pair):
        high, middle, parts = finish(across[pair], gram[pair], square[pair], obs[pair])
        out_ref[pair, 2 * size :] = parts
        for first, part in ((0, high), (size, middle)):
            turn[...] = part
            for n in range(tile_count):
                place = pl.ds(pl.multiple_of(meta_ref[n] * pair_rows, pair_rows), pair_rows)
                out_ref[pair, first + n * pair_rows : first + (n + 1) * pair_rows] = turn[place, :]


def pair_matrices(slots, shard, first_pair, arc_of_row, autoreg, movavg, pair_rows):
    tile_count = sum(slot.shape[0] for slot in slots)
    rows, width = slots[0].shape[1:]
    param_count = width // 2
    pair_count = rows // pair_rows
    size = tile_count * pair_rows
    meta = jnp.concatenate([shard, jnp.reshape(first_pair, (1,)).astype(jnp.int32)])
    first = 2 * jnp.arange(autoreg.shape[0] // 2, dtype=jnp.int32)
    lengths = jnp.sum((arc_of_row == first[None, :]).astype(jnp.int32), axis=0)
    return pl.pallas_call(
        pair_kernel,
        in_specs=[SMEM] * 4 + [pl.BlockSpec(memory_space=pltpu.VMEM)] * len(slots),
        out_specs=pl.BlockSpec(memory_space=pltpu.VMEM),
        out_shape=jax.ShapeDtypeStruct((pair_count, 2 * size + EXTRA, size), jnp.bfloat16),
        scratch_shapes=[
            pltpu.VMEM((size, width), jnp.float32),
            pltpu.VMEM((pair_count, param_count, width), jnp.float32),
            pltpu.VMEM((pair_count, width, size), jnp.float32),
            pltpu.VMEM((pair_count, size, size), jnp.float32),
            pltpu.VMEM((pair_count, EXTRA, size), jnp.bfloat16),
            pltpu.VMEM((size, size), jnp.bfloat16),
        ],
        compiler_params=params(58),
        cost_estimate=cost(SMALL * 2),
        name="pair_matrices",
    )(meta, lengths, autoreg + movavg, jnp.log(movavg), *slots)


def pack_kernel(parts, width, meta_ref, *refs):
    count = 1 + max(slot for part in parts for slot in part)
    slots, outs, held, sems = refs[:count], refs[count:-2], refs[-2], refs[-1]

    @pl.when(meta_ref[0] == 1)
    def _():
        into, back, row = [], [], 0
        for which, (part, out) in enumerate(zip(parts, outs)):
            start, at = pl.multiple_of(meta_ref[1 + which], 128), 0
            for slot in part:
                rows, n = slots[slot].shape[0], len(into)
                here = held.at[pl.ds(row, rows)]
                columns = slots[slot].at[:, pl.ds(start, width)]
                into.append(pltpu.make_async_copy(columns, here, sems.at[0, n]))
                back.append(pltpu.make_async_copy(here, out.at[pl.ds(at, rows)], sems.at[1, n]))
                at, row = at + rows, row + rows
        for copy in into:
            copy.start()
        for first, second in zip(into, back):
            first.wait()
            second.start()
        for copy in back:
            copy.wait()


def pack(meta, slots, parts, width):
    rows = [sum(slots[slot].shape[0] for slot in part) for part in parts]
    copies = sum(len(part) for part in parts)
    return pl.pallas_call(
        functools.partial(pack_kernel, tuple(parts), width),
        in_specs=[SMEM] + [HBM] * len(slots),
        out_specs=[HBM] * len(parts),
        out_shape=[jax.ShapeDtypeStruct((count, width), slots[0].dtype) for count in rows],
        scratch_shapes=[
            pltpu.VMEM((sum(rows), width), slots[0].dtype),
            pltpu.SemaphoreType.DMA((2, copies)),
        ],
        cost_estimate=cost(SMALL * 2),
        name="pack",
    )(meta, *slots)


def middle_rows_kernel(count, scale, step, meta_ref, *refs):
    mids, slots, (out, rhs, panel, held, sems) = refs[:2], refs[2:-5], refs[-5:]
    pair_rows, width = slots[0].shape
    size = count * pair_rows
    pair, pairs = pl.program_id(0), held.shape[0]
    core = meta_ref[count]

    def fetch(which, kind):
        source = mids[kind].at[which % (pairs // 2)]
        return pltpu.make_async_copy(source, held.at[which], sems.at[which])

    @pl.when(pair == 0)
    def _():
        rhs[...] = jnp.zeros_like(rhs)
        for mine in range(2):

            @pl.when(core == mine)
            def _(mine=mine):
                for which in range(pairs):
                    fetch(which, int(which // (pairs // 2) != mine)).start()

    places = [
        pl.ds(pl.multiple_of(meta_ref[n] * pair_rows, pair_rows), pair_rows) for n in range(count)
    ]
    for place, slot in zip(places, slots[: count - 1]):
        panel[place, :] = slot[...]

    @pl.when(pair < pairs // 2)
    def _():
        panel[places[-1], :] = slots[-2][...]

    @pl.when(pair >= pairs // 2)
    def _():
        panel[places[-1], :] = slots[-1][...]

    fetch(pair, 0).wait()
    for at in range(0, width, step):
        here = slice(at, min(at + step, width))
        product = jnp.dot(held[pair], panel[:, here], preferred_element_type=jnp.float32)
        middle = (product[:size] + product[size : 2 * size]).astype(jnp.bfloat16)
        for n in range(count):
            out[n, :, here] = middle[n * pair_rows : (n + 1) * pair_rows]
        rhs[:, here] += jnp.sum(product[2 * size :], axis=0, keepdims=True) * scale


def middle_rows(meta, mids, slots, pair_rows, scale, step):
    rows, width = slots[0].shape
    pair_count, size, columns = rows // pair_rows, mids[0].shape[2], mids[0].shape[1]
    count = len(slots) - 1
    half = pair_count // 2
    slot_specs = [pl.BlockSpec((pair_rows, width), lambda b: (b, 0))] * (count - 1)
    slot_specs += [
        pl.BlockSpec((pair_rows, width), lambda b: (jnp.minimum(b, half - 1), 0)),
        pl.BlockSpec((pair_rows, width), lambda b: (jnp.maximum(b - half, 0), 0)),
    ]
    return pl.pallas_call(
        functools.partial(middle_rows_kernel, count, scale, step),
        grid=(pair_count,),
        in_specs=[SMEM] + [HBM] * 2 + slot_specs,
        out_specs=[
            pl.BlockSpec((count, pair_rows, width), lambda b: (0, b, 0)),
            pl.BlockSpec((1, width), lambda b: (0, 0)),
        ],
        out_shape=[
            jax.ShapeDtypeStruct((count, rows, width), jnp.bfloat16),
            jax.ShapeDtypeStruct((1, width), jnp.float32),
        ],
        scratch_shapes=[
            pltpu.VMEM((size, width), jnp.bfloat16),
            pltpu.VMEM((pair_count, columns, size), jnp.bfloat16),
            pltpu.SemaphoreType.DMA((pair_count,)),
        ],
        compiler_params=params(48),
        cost_estimate=cost(ROWS),
        name="middle_rows",
    )(meta, *mids, *slots)


def collect_kernel(slot_places, over_places, slot_count, meta_ref, *refs):
    slots, overs, (out, held, turned, sems) = refs[:slot_count], refs[slot_count:-4], refs[-4:]
    offset = pl.multiple_of(meta_ref[3], 64)
    width = held.shape[1]
    rows = held.shape[0] // len(slot_places)
    start = pl.multiple_of(meta_ref[2], 128)

    def copies(near):
        found = []
        for n in range(len(slot_places)):
            which, at = slot_places[n] if near else over_places[n]
            ref = slots[which].at[pl.ds(at, rows), pl.ds(start, width)] if near else overs[which].at[pl.ds(at, rows)]
            found.append(pltpu.make_async_copy(ref, held.at[pl.ds(n * rows, rows)], sems.at[n]))
        return found

    for near in (True, False):

        @pl.when((meta_ref[0] == 1) & (meta_ref[1] == int(near)))
        def _(near=near):
            for copy in copies(near):
                copy.start()
            for n, copy in enumerate(copies(near)):
                copy.wait()
                turned[...] = held[n * rows : (n + 1) * rows, :].T
                out[:, n * rows : (n + 1) * rows] = turned[pl.ds(offset, out.shape[0]), :]


def collect(meta, slots, slot_places, overs, over_places, rows, width, block_columns):
    total = rows * len(slot_places)
    return pl.pallas_call(
        functools.partial(collect_kernel, tuple(slot_places), tuple(over_places), len(slots)),
        in_specs=[SMEM] + [HBM] * (len(slots) + len(overs)),
        out_specs=pl.BlockSpec(memory_space=pltpu.VMEM),
        out_shape=jax.ShapeDtypeStruct((block_columns, total), jnp.bfloat16),
        scratch_shapes=[
            pltpu.VMEM((total, width), jnp.bfloat16),
            pltpu.VMEM((width, rows), jnp.bfloat16),
            pltpu.SemaphoreType.DMA((len(slot_places),)),
        ],
        compiler_params=params(24),
        cost_estimate=cost(SMALL * 2),
        name="collect",
    )(meta, *slots, *overs)


def tile_kernel(scale, meta_ref, *refs):
    blocks, (middle_ref, out, block, sems) = refs[:4], refs[4:]

    def copies(kind):
        found, at = [], 0
        for n, ref in enumerate(blocks[2 * kind : 2 * kind + 2]):
            count = ref.shape[1]
            found.append(pltpu.make_async_copy(ref, block.at[:, pl.ds(at, count)], sems.at[n]))
            at += count
        return found

    @pl.when(pl.program_id(0) == 0)
    def _():
        for kind in range(2):

            @pl.when(meta_ref[0] != kind)
            def _(kind=kind):
                for copy in copies(kind):
                    copy.start()

        for copy in copies(0):
            copy.wait()

    middle = middle_ref[...].reshape(-1, middle_ref.shape[2])
    out[...] = jnp.dot(block[...], middle, preferred_element_type=jnp.float32) * scale


def tile(meta, middle, blocks, scale, step):
    count, rows, width = middle.shape
    block_columns = blocks[0].shape[0]
    return pl.pallas_call(
        functools.partial(tile_kernel, scale),
        grid=(pl.cdiv(width, step),),
        in_specs=[SMEM] + [HBM] * 4 + [pl.BlockSpec((count, rows, step), lambda j: (0, 0, j))],
        out_specs=pl.BlockSpec((block_columns, step), lambda j: (0, j)),
        out_shape=jax.ShapeDtypeStruct((block_columns, width), jnp.float32),
        scratch_shapes=[
            pltpu.VMEM((block_columns, count * rows), jnp.bfloat16),
            pltpu.SemaphoreType.DMA((2,)),
        ],
        compiler_params=params(48),
        cost_estimate=cost(12),
        name="tile",
    )(meta, *blocks, middle)


def tie(value, *others):
    return lax.optimization_barrier((value, *others))[0]


def block_body(design, partials, observed, arc_of_row, autoreg, movavg):
    tile_count, panel_count = lax.axis_size("tm"), lax.axis_size("panel")
    rows_dev, width = design.shape
    block_columns = width * panel_count // tile_count
    payload = pl.cdiv(block_columns, 128) * 128
    pair_rows = 2 * rows_dev // tile_count
    scale = 1.0 / (rows_dev * tile_count)
    t, p = lax.axis_index("tm"), lax.axis_index("panel")
    z, x, y, core = t // 2, t % 2, p // 2, p % 2
    near, same_core = y == z // 2, core == z % 2

    def along_z(value, turn):
        pairs = [(2 * s + i, 2 * d + i) for s, d in SEND_Z[turn] for i in range(2)]
        return lax.ppermute(value, "tm", pairs)

    def across_x(value):
        return lax.ppermute(value, "tm", [(s, s ^ 1) for s in range(tile_count)])

    def hop(value, go):
        pairs = []
        for s in range(tile_count * panel_count):
            sz, sy, sc = s // 8, s // 2 % 2, s % 2
            to = go(sy == sz // 2, sc == sz % 2)
            if to is not None:
                pairs.append((s, s - s % 4 + (sy ^ to[0]) * 2 + (sc ^ to[1])))
        return lax.ppermute(value, AXES, pairs)

    line = [z] + [lax.rem((turn + 2) * z + turn + 1, 5) for turn in range(3)]
    shard = jnp.stack([2 * s + i for s in line for i in (x, 1 - x)]).astype(jnp.int32)

    half = rows_dev // 2
    pairs = half // pair_rows
    sent = jnp.concatenate([partials, jnp.broadcast_to(observed[:, None], partials.shape)], axis=1)
    sent = jnp.where(core == 0, sent[:half], sent[half:])
    both = jnp.stack([sent, across_x(sent)])
    sent_z = [both] + [along_z(both, turn) for turn in (0, 1, 3)]
    z1 = along_z(design, 0)
    x0 = across_x(tie(design, both))
    sent_z[0] = tie(sent_z[0], z1, x0)
    mid = pair_matrices(sent_z, shard, core * pairs, arc_of_row, autoreg, movavg, pair_rows)

    start = x * (width - payload)
    sends = (near & same_core).astype(jnp.int32)

    def picked(start, *slots):
        return pack(jnp.stack([sends, start]), slots, (tuple(range(len(slots))),), payload)[0]

    def over(value):
        return hop(value, lambda near, same: (1, 0) if near and same else None)

    def beside(value):
        return hop(value, lambda near, same: (0, 1) if same else None)

    z2 = along_z(tie(design, z1, x0, *sent_z), 1)
    x1 = across_x(tie(z1, x0))
    picked_0 = picked(start, design, x0, z1)
    z3 = along_z(tie(z1, z2, x1, mid, picked_0), 2)
    x2 = across_x(tie(z2, x1))
    x1_half = x1[:half]
    picked_1 = picked(start, x1, tie(z2, mid, x1_half))
    mids = (mid, hop(mid, lambda near, same: (0, 1)))
    slots_meta = jnp.concatenate([shard, core[None]])
    last_a = along_z(tie(x1_half, z3, x2), 2)
    last_b = across_x(tie(z3[half:], x2, picked_0, picked_1))
    across = (1 - x) * (width - payload)
    picked_3, picked_2 = pack(jnp.stack([sends, across, start]), (x2, z3), ((1,), (0, 1)), payload)
    over_0, over_1, over_2 = over(picked_0), over(picked_1), over(picked_2)
    over_3 = across_x(tie(over(picked_3), last_b, last_a))

    block_meta = jnp.stack(
        [same_core.astype(jnp.int32), near.astype(jnp.int32), start, x * (payload - block_columns)]
    )
    early = collect(
        block_meta,
        (design, x0, z1, x1, z2),
        [(n, 0) for n in range(5)],
        (over_0, over_1),
        [(n // 3, n % 3 * rows_dev) for n in range(5)],
        rows_dev,
        payload,
        block_columns,
    )
    slots = (design, x0, z1, x1, z2, x2, z3, last_a, tie(last_b, early))
    middle, rhs = middle_rows(slots_meta, mids, slots, pair_rows, scale, 512)
    late = collect(
        block_meta,
        (x2, z3, last_a, tie(last_b, rhs)),
        [(0, 0), (0, half), (1, 0), (1, half), (2, 0), (3, 0)],
        (over_2, over_3),
        [(n // 4, n % 4 * half) for n in range(6)],
        half,
        payload,
        block_columns,
    )
    blocks = (early, late, beside(early), beside(late))
    normal = tile(block_meta, middle, blocks, scale, 512)
    return normal, rhs[0]


def line_body(design, partials, observed, arc_of_row, autoreg, movavg):
    tile_count = lax.axis_size("tm")
    rows_dev, width = design.shape
    pair_rows = 2 * rows_dev // tile_count
    pair_count = rows_dev // pair_rows
    size = tile_count * pair_rows
    scale = 1.0 / (rows_dev * tile_count)
    sent = jnp.concatenate([partials, jnp.broadcast_to(observed[:, None], partials.shape)], axis=1)
    sent = lax.all_gather(sent, "tm", axis=0, tiled=False)
    shard = jnp.arange(tile_count, dtype=jnp.int32)
    mids = pair_matrices([sent], shard, 0, arc_of_row, autoreg, movavg, pair_rows)
    panel = lax.all_gather(design, "tm", axis=0, tiled=False)
    whole_rows = lax.all_gather(design, "panel", axis=1, tiled=True)
    block = lax.all_to_all(whole_rows, "tm", split_axis=1, concat_axis=0, tiled=True)
    block = block.reshape(tile_count, rows_dev, -1)

    def one_pair(sums, pair):
        def rows_of(values):
            here = lax.dynamic_slice_in_dim(values, pair * pair_rows, pair_rows, 1)
            return here.reshape(size, values.shape[2])

        product = jnp.dot(mids[pair], rows_of(panel), preferred_element_type=jnp.float32)
        middle = (product[:size] + product[size : 2 * size]).astype(jnp.bfloat16)
        here = lax.dot_general(
            rows_of(block), middle, ROWS_ACROSS, preferred_element_type=jnp.float32
        )
        return (sums[0] + here, sums[1] + jnp.sum(product[2 * size :], axis=0)), None

    start = (jnp.zeros((block.shape[2], width), jnp.float32), jnp.zeros((width,), jnp.float32))
    (normal, right_hand), _ = lax.scan(one_pair, start, jnp.arange(pair_count))
    return normal * scale, right_hand * scale


def solution(mesh):
    in_specs = (P("tm", "panel"), P("tm", None), P("tm"), P(), P(), P())
    out_specs = (P("tm", "panel"), P("panel"))
    body = block_body if (mesh.shape["tm"], mesh.shape["panel"]) == (8, 4) else line_body
    return jax.shard_map(body, mesh=mesh, in_specs=in_specs, out_specs=out_specs, check_vma=False)
```
